512 devices in a mesh: section: 8 (over y, x_lo), tp: 64 (over z, x_hi, core).
Axes of the slice: x: 4 (x_hi: 2, x_lo: 2; x = x_hi * 2 + x_lo), y: 4, z: 16, core: 2. Of those that a mesh axis runs over, the one named last changes fastest.
Arguments:
- hidden_in: bfloat16 [8, 8, 4096], P('section', None, 'tp'), may hold values from -6 to 6
- norm_gain: float32 [8, 4096], P('section'), may hold values from 0.25 to 1.75
- w_qkv: bfloat16 [8, 4096, 6144], P('section', None, 'tp'), may hold values from -0.09375 to 0.09375
- w_out: bfloat16 [8, 4096, 4096], P('section', None, 'tp'), may hold values from -0.09375 to 0.09375
- paged_key_codes: bfloat16 [8, 512, 64, 1024], P('section', 'tp'), may hold values from -127 to 127, as said below
- paged_value_codes: bfloat16 [8, 512, 64, 1024], P('section', 'tp'), may hold values from -127 to 127, as said below
- paged_scale_table: float32 [8, 512, 2, 8], P('section', 'tp'), may hold values from 0.005 to 1
- page_owner: int32 [8, 512], P('section', 'tp'), may hold values from 0 to 16, as said below
- page_pos: int32 [8, 512], P('section', 'tp'), may hold values from 0 to 127, as said below
- lengths: int32 [8, 16], P('section'), may hold values from 1 to 8192, as said below
- row_assign: int32 [8, 8], P('section'), may hold values from 0 to 15, as said below
Outputs:
- hidden_out: float32 [8, 8, 4096], P('section', None, 'tp')
The draws below stay inside these ranges and needn't reach their ends.
Inputs may be any that keep to these rules, and one draw needn't show every extreme that they name: `paged_key_codes`: whole numbers. `paged_value_codes`: whole numbers. `page_owner`: A slot holding 16 is free; every section has a free slot, and every request holds at least one page. `page_pos`: the slots of one request carry its page numbers 0, 1, ... up to its page count minus one, each once; a free slot carries 0. One request of every section holds 128 pages. `lengths`: A request holding n pages has a length from (n - 1) * 64 + 1 to n * 64; the request holding 128 pages has length 8192. `row_assign`: the rows of one section name distinct requests, request 16 - 1 among them.
All inputs are finite; a program needn't handle non-finite values.
Results may differ from the reference program's by a relative error of at most 0.014.
The reference program's roundings to bfloat16 on the way count: a program that leaves them out, or rounds other values in their place, can miss the bound.
Values may be sent and summed in bfloat16 or wider, within the bound.
A program may use at most 64 MiB of HBM per device.

```python
import math
import jax
import jax.numpy as jnp
from jax import lax

D = 4096
QUERY_HEADS = 32
KEY_VALUE_HEADS = 8
HEAD_SIZE = 128
BATCH_REQUESTS = 8
PAGE_TOKENS = 64
QUERY_WIDTH = 4096
KEY_TOKEN_WIDTH = 1024
QKV = 6144
REQS = 16
SECTION_SLOTS = 512
N_SECTION = 8


def section_table(key):
    longest = SECTION_SLOTS // 4
    limit = min(longest, (SECTION_SLOTS - longest - 1) // (REQS - 1))
    request_ids = jnp.arange(REQS, dtype=jnp.int32)
    chosen = jax.random.randint(jax.random.fold_in(key, 21), (), 0, REQS)
    first = jax.random.randint(jax.random.fold_in(key, 22), (REQS,), 0, limit)
    second = jax.random.randint(jax.random.fold_in(key, 23), (REQS,), 0, limit)
    counts = 1 + first * second // limit
    counts = jnp.where(request_ids == chosen, longest, counts).astype(jnp.int32)
    starts = jnp.cumsum(counts) - counts
    virtual = jnp.arange(SECTION_SLOTS, dtype=jnp.int32)
    inside = (virtual[:, None] >= starts[None, :]) & (virtual[:, None] < (starts + counts)[None, :])
    owner = jnp.sum(jnp.where(inside, request_ids[None, :], 0), axis=1) + jnp.where(jnp.any(inside, axis=1), 0, REQS)
    number = jnp.sum(jnp.where(inside, virtual[:, None] - starts[None, :], 0), axis=1)
    order = jax.random.permutation(jax.random.fold_in(key, 24), SECTION_SLOTS)
    owner = owner[order]
    number = number[order]
    tail = jax.random.randint(jax.random.fold_in(key, 25), (REQS,), 1, PAGE_TOKENS + 1)
    tail = jnp.where(request_ids == chosen, PAGE_TOKENS, tail)
    section_lengths = (counts - 1) * PAGE_TOKENS + tail
    return (owner.astype(jnp.int32), number.astype(jnp.int32), section_lengths.astype(jnp.int32))


def page_tables(key):
    key_rows = jax.random.split(jax.random.fold_in(key, 20), N_SECTION)
    return jax.vmap(section_table)(key_rows)


def summed_codes(key, target_shape):
    drawn = jax.random.randint(key, target_shape, 0, 87 * 87 * 87)
    first = drawn % 87
    second = drawn // 87 % 87
    third = drawn // 7569 % 87
    return jnp.clip(first + second + third - 129, -127, 127)


def draw_page_owner(key, part):
    tables = page_tables(key)
    return tables[0]


def draw_page_pos(key, part):
    tables = page_tables(key)
    return tables[1]


def draw_lengths(key, part):
    tables = page_tables(key)
    return tables[2]


def draw_row_assign(key, part):
    key = jax.random.fold_in(key, 4)
    key_rows = jax.random.split(key, N_SECTION)

    def pick_rows(single):
        picked = jax.random.permutation(jax.random.fold_in(single, 1), REQS)[:BATCH_REQUESTS].astype(jnp.int32)
        present = jnp.any(picked == REQS - 1)
        place = jax.random.randint(jax.random.fold_in(single, 2), (), 0, BATCH_REQUESTS)
        replace = (jnp.arange(BATCH_REQUESTS, dtype=jnp.int32) == place) & jnp.logical_not(present)
        return jnp.where(replace, REQS - 1, picked)
    return jax.vmap(pick_rows)(key_rows).astype(jnp.int32)


def draw_paged_key_codes(key, part):
    key = jax.random.fold_in(key, 5)
    target_shape = (N_SECTION, SECTION_SLOTS, PAGE_TOKENS, KEY_TOKEN_WIDTH)
    stored_codes = summed_codes(key, target_shape)
    return stored_codes.astype(jnp.float32).astype(jnp.bfloat16)


def draw_paged_value_codes(key, part):
    key = jax.random.fold_in(key, 6)
    target_shape = (N_SECTION, SECTION_SLOTS, PAGE_TOKENS, KEY_TOKEN_WIDTH)
    stored_codes = summed_codes(key, target_shape)
    return stored_codes.astype(jnp.float32).astype(jnp.bfloat16)


def draw_paged_scale_table(key, part):
    key = jax.random.fold_in(key, 7)
    target_shape = (N_SECTION, SECTION_SLOTS, KEY_VALUE_HEADS)
    key_scale = jnp.exp(jax.random.uniform(jax.random.fold_in(key, 1), target_shape, jnp.float32, math.log(0.005), math.log(1.0)))
    value_scale = jnp.exp(jax.random.uniform(jax.random.fold_in(key, 2), target_shape, jnp.float32, math.log(0.006), math.log(0.06)))
    return jnp.stack([key_scale, value_scale], axis=2).astype(jnp.float32)


def levels(key, shape, shards, low, largest):
    level = 1.0
    for position, blocks in shards:
        heights = jax.random.uniform(jax.random.fold_in(jax.random.fold_in(key, 6), position), (blocks,), jnp.float32, low / len(shards), largest / len(shards))
        level = level * jnp.repeat(jnp.exp(heights), shape[position] // blocks).reshape((-1,) + (1,) * (len(shape) - 1 - position))
    return level


def scatter_about(rng, shape, deviation, reach, cuts=(), kind=jnp.bfloat16):
    gain = levels(rng, shape, cuts, -0.22, 0.18) if cuts else 1.0
    entries = jax.random.normal(rng, shape, jnp.float32) * deviation * gain
    return jnp.minimum(jnp.maximum(entries, -reach), reach).astype(kind)


def setup_inputs(seed: int = 0) -> dict:
    splits = jax.random.split(jax.random.key(seed), 12)
    return {
        "hidden_in": scatter_about(splits[0], (N_SECTION, BATCH_REQUESTS, D), 1.0, 6.0, ((0, 8), (2, 64))),
        "norm_gain": jnp.clip(1.0 + 0.15 * jax.random.normal(splits[1], (N_SECTION, D), jnp.float32), 0.25, 1.75),
        "w_qkv": scatter_about(splits[2], (N_SECTION, D, QKV), D ** -0.5, 0.09375, ((0, 8), (2, 64))),
        "w_out": scatter_about(splits[3], (N_SECTION, QUERY_WIDTH, D), QUERY_WIDTH ** -0.5, 0.09375, ((0, 8), (2, 64))),
        "paged_key_codes": draw_paged_key_codes(jax.random.fold_in(splits[11], 71), 0),
        "paged_value_codes": draw_paged_value_codes(jax.random.fold_in(splits[11], 71), 0),
        "paged_scale_table": draw_paged_scale_table(jax.random.fold_in(splits[11], 71), 0),
        "page_owner": draw_page_owner(jax.random.fold_in(splits[11], 71), 0),
        "page_pos": draw_page_pos(jax.random.fold_in(splits[11], 71), 0),
        "lengths": draw_lengths(jax.random.fold_in(splits[11], 71), 0),
        "row_assign": draw_row_assign(jax.random.fold_in(splits[11], 71), 0),
    }


rope_base = 500000.0

def apply_rotation(heads, token_position):
    half = heads.shape[-1] // 2
    freq = rope_base ** (-jnp.arange(half, dtype=jnp.float32) / half)
    angle = token_position.astype(jnp.float32)[:, None, None] * freq[None, None, :]
    cosine = jnp.cos(angle)
    sine = jnp.sin(angle)
    first = heads[..., :half]
    second = heads[..., half:]
    return jnp.concatenate([first * cosine - second * sine, second * cosine + first * sine], axis=-1)

def restore_codes(stored_codes, scales):
    reshaped_rows = stored_codes.astype(jnp.float32).reshape(stored_codes.shape[0], PAGE_TOKENS, KEY_VALUE_HEADS, HEAD_SIZE)
    return (reshaped_rows * scales[:, None, :, None]).astype(jnp.bfloat16).reshape(stored_codes.shape[0] * PAGE_TOKENS, KEY_TOKEN_WIDTH)

def reference(hidden_in, norm_gain, w_qkv, w_out, paged_key_codes, paged_value_codes, paged_scale_table, page_owner, page_pos, lengths, row_assign):
    query_group = QUERY_HEADS // KEY_VALUE_HEADS
    inverse_square_root = 1.0 / HEAD_SIZE ** 0.5
    results = []
    for section in range(N_SECTION):
        page_holder = (section - 1) % N_SECTION
        x_rows = hidden_in[page_holder]
        widened = x_rows.astype(jnp.float32)
        normed = (widened * lax.rsqrt(lax.optimization_barrier(jnp.mean(widened * widened, axis=-1, keepdims=True)) + 1e-05) * norm_gain[section][None, :]).astype(jnp.bfloat16)
        query_key_value = jnp.dot(normed, w_qkv[section], preferred_element_type=jnp.float32).astype(jnp.bfloat16)
        lengths_here = lengths[page_holder]
        rows_here = row_assign[page_holder]
        token_position = jnp.take(lengths_here, rows_here.astype(jnp.int32))
        query_rows = apply_rotation(query_key_value[:, :QUERY_WIDTH].astype(jnp.float32).reshape(BATCH_REQUESTS, QUERY_HEADS, HEAD_SIZE), token_position).astype(jnp.bfloat16)
        fresh_key = apply_rotation(query_key_value[:, QUERY_WIDTH:QUERY_WIDTH + KEY_TOKEN_WIDTH].astype(jnp.float32).reshape(BATCH_REQUESTS, KEY_VALUE_HEADS, HEAD_SIZE), token_position).astype(jnp.bfloat16)
        fresh_value = query_key_value[:, QUERY_WIDTH + KEY_TOKEN_WIDTH:].reshape(BATCH_REQUESTS, KEY_VALUE_HEADS, 1, HEAD_SIZE).astype(jnp.float32)
        key_rows = restore_codes(paged_key_codes[page_holder], paged_scale_table[page_holder][:, 0]).astype(jnp.float32).reshape(-1, KEY_VALUE_HEADS, HEAD_SIZE)
        value_matrix = restore_codes(paged_value_codes[page_holder], paged_scale_table[page_holder][:, 1]).astype(jnp.float32).reshape(-1, KEY_VALUE_HEADS, HEAD_SIZE)
        tok_owner = jnp.repeat(page_owner[page_holder], PAGE_TOKENS)
        tok_pos = (page_pos[page_holder][:, None] * PAGE_TOKENS + jnp.arange(PAGE_TOKENS, dtype=jnp.int32)[None, :]).reshape(-1)
        mask = (tok_owner[None, :] == rows_here[:, None]) & (tok_pos[None, :] < token_position[:, None])
        heads_of_queries = query_rows.astype(jnp.float32).reshape(BATCH_REQUESTS, KEY_VALUE_HEADS, query_group, HEAD_SIZE)
        scores = jnp.einsum('rgqd,tgd->rgqt', heads_of_queries, key_rows) * inverse_square_root
        masked = jnp.where(mask[:, None, None, :], scores, -1e+30)
        owned_pages = lax.optimization_barrier(jnp.sum(heads_of_queries * fresh_key.astype(jnp.float32).reshape(BATCH_REQUESTS, KEY_VALUE_HEADS, 1, HEAD_SIZE), axis=-1)) * inverse_square_root
        peak = jnp.maximum(lax.optimization_barrier(jnp.max(masked, axis=-1)), owned_pages)
        weights = jnp.where(mask[:, None, None, :], jnp.exp(masked - peak[..., None]), 0.0)
        total = lax.optimization_barrier(jnp.sum(weights, axis=-1))
        weighted = jnp.einsum('rgqt,tgd->rgqd', weights.astype(jnp.bfloat16).astype(jnp.float32), value_matrix)
        own_weight = jnp.exp(owned_pages - peak)
        attended = ((weighted + own_weight[..., None] * fresh_value) / (total + own_weight)[..., None]).astype(jnp.bfloat16).reshape(BATCH_REQUESTS, QUERY_WIDTH)
        output = jnp.dot(attended, w_out[section], preferred_element_type=jnp.float32) + widened
        results.append(output.astype(jnp.float32))
    return jnp.stack(results, axis=0)
```

```python
import functools

import jax
import jax.numpy as jnp
import numpy as np
from jax import lax
from jax.experimental import pallas as pl
from jax.experimental.pallas import tpu as pltpu
from jax.sharding import PartitionSpec as P

MESH = pl.DeviceIdType.MESH
F32, BF16, I32 = jnp.float32, jnp.bfloat16, jnp.int32

ROWS = 8
HEAD = 128
QUERY_HEADS = 32
KEY_HEADS = 8
HEADS = QUERY_HEADS + 2 * KEY_HEADS
PAGE = 64
BLOCKS = 4
NEAR = 16
SLOTS = 8
TOKENS = SLOTS * PAGE
SCALE = 1.0 / HEAD**0.5
MASKED = -1e30
LOWEST = -1e25
ROPE_BASE = 500000.0
X_FAR, X_NEAR, Q_FAR, Q_NEAR, PART_NEAR, PART_FAR, OUT_NEAR = range(7)


def nt(left, right):
    return lax.dot_general(
        left, right, (((1,), (1,)), ((), ())), preferred_element_type=F32
    )


def thirds(value):
    first = value.astype(BF16).astype(F32)
    rest = value - first
    second = rest.astype(BF16).astype(F32)
    return first, second, rest - second


def pack_stats(top, total, shape):
    lane = lax.broadcasted_iota(I32, shape, 1)
    pieces = thirds(top) + thirds(total)
    tile = jnp.broadcast_to(pieces[5], shape)
    for k in range(4, -1, -1):
        tile = jnp.where(lane < 16 * (k + 1), jnp.broadcast_to(pieces[k], shape), tile)
    return tile.astype(BF16)


def unpack_stats(tile):
    wide = tile.astype(F32)
    part = [wide[:, 16 * k : 16 * k + 1] for k in range(6)]
    return part[0] + part[1] + part[2], part[3] + part[4] + part[5]


def merge(tops, totals, sums):
    top = functools.reduce(jnp.maximum, tops)
    total, weighted = 0.0, 0.0
    for t, l, a in zip(tops, totals, sums):
        factor = jnp.exp(t - top)
        total = total + factor * l
        weighted = weighted + factor * a
    return top, total, weighted


def kernel(
    x_hbm,
    gain_hbm,
    wq_hbm,
    wo_hbm,
    key_hbm,
    value_hbm,
    scale_hbm,
    owner_hbm,
    number_hbm,
    length_hbm,
    row_hbm,
    freq_hbm,
    out_ref,
    x_own,
    gain,
    wq,
    wo,
    keys,
    values,
    scales,
    owner,
    number,
    length,
    row,
    freq,
    bias,
    turn,
    x_send,
    x_far,
    x_pack,
    x_all,
    q_send,
    q_far,
    q_all,
    heads,
    part_send,
    part_all,
    sum_send,
    sum_all,
    att_send,
    att_all,
    local_sem,
    send_sem,
    recv_sem,
):
    section = lax.axis_index("section")
    tp = lax.axis_index("tp")
    block, mine = tp // NEAR, tp % NEAR
    sections = lax.axis_size("section")
    after = lax.rem(section + 1, sections)
    before = lax.rem(section + sections - 1, sections)

    def near(d):
        return lax.rem(mine + d, NEAR)

    def near_id(other):
        return {"tp": block * NEAR + other}

    def far_id(where, other):
        return {"section": where, "tp": other * NEAR + mine}

    barrier = pltpu.get_barrier_semaphore()

    def greet_near(d, carry):
        pl.semaphore_signal(barrier, inc=1, device_id=near_id(near(d)), device_id_type=MESH)
        return carry

    def greet_far(d, carry):
        other = lax.rem(block + d, BLOCKS)
        pl.semaphore_signal(barrier, inc=1, device_id=far_id(after, other), device_id_type=MESH)
        pl.semaphore_signal(barrier, inc=1, device_id=far_id(before, other), device_id_type=MESH)
        return carry

    lax.fori_loop(0, BLOCKS, greet_far, 0)
    lax.fori_loop(1, NEAR, greet_near, 0)

    moves = [
        pltpu.make_async_copy(src, dst, local_sem.at[k])
        for k, (src, dst) in enumerate(
            [
                (x_hbm, x_own),
                (row_hbm, row),
                (length_hbm, length),
                (owner_hbm, owner),
                (number_hbm, number),
                (scale_hbm, scales),
                (freq_hbm, freq),
                (key_hbm, keys),
                (value_hbm, values),
                (gain_hbm, gain),
                (wq_hbm, wq.at[pl.ds(0, 96)]),
                (wo_hbm, wo),
            ]
        )
    ]
    for move in moves:
        move.start()
    wq[96:128, :] = jnp.zeros((32, wq.shape[1]), BF16)

    moves[0].wait()
    x_here = x_own[...].astype(F32)
    x_send[...] = jnp.concatenate([x_here, x_here], axis=1).astype(BF16)

    for k in range(1, 7):
        moves[k].wait()
    lane = lax.broadcasted_iota(I32, (ROWS, HEAD), 1)
    sub = lax.broadcasted_iota(I32, (ROWS, HEAD), 0)
    low = lane < HEAD // 2
    row_of = jnp.zeros((ROWS, HEAD), I32)
    limit = jnp.zeros((ROWS, HEAD), I32)
    for r in range(ROWS):
        request = row[0, r]
        row_of = jnp.where(sub == r, request, row_of)
        limit = jnp.where(sub == r, length[0, request], limit)
    for j in range(SLOTS // 2):
        tok_owner = jnp.where(low, owner[0, 2 * j], owner[0, 2 * j + 1])
        tok_page = jnp.where(low, number[0, 2 * j], number[0, 2 * j + 1])
        tok_pos = tok_page * PAGE + lane % PAGE
        seen = (tok_owner == row_of) & (tok_pos < limit)
        bias[:, HEAD * j : HEAD * (j + 1)] = jnp.where(seen, 0.0, MASKED)
    angle = limit.astype(F32) * freq[...]
    turn[0] = jnp.cos(angle)
    sine = jnp.sin(angle)
    turn[1] = jnp.where(low, -sine, sine)

    moves[7].wait()
    moves[8].wait()

    def restore(k, carry):
        at = pl.ds(pl.multiple_of(k * PAGE, PAGE), PAGE)
        both = scales[k]
        for which, store in ((0, keys), (1, values)):
            for g in range(KEY_HEADS):
                cols = pl.ds(g * HEAD, HEAD)
                factor = jnp.broadcast_to(both[which : which + 1, g : g + 1], (PAGE, HEAD))
                store[at, cols] = (store[at, cols].astype(F32) * factor).astype(BF16)
        return carry

    lax.fori_loop(0, SLOTS, restore, 0)
    moves[9].wait()
    moves[10].wait()
    moves[11].wait()

    def start_far(stage, where, src, dst):
        def go(d, carry):
            other = lax.rem(block + BLOCKS // 2 + d, BLOCKS)
            pltpu.make_async_remote_copy(
                src_ref=src,
                dst_ref=dst.at[block],
                send_sem=send_sem.at[stage],
                recv_sem=recv_sem.at[stage],
                device_id=far_id(where, other),
                device_id_type=MESH,
            ).start()
            return carry

        lax.fori_loop(0, BLOCKS, go, 0)

    def start_near(stage, src_of, dst):
        def go(d, carry):
            other = near(d)
            pltpu.make_async_remote_copy(
                src_ref=src_of(other),
                dst_ref=dst.at[mine],
                send_sem=send_sem.at[stage],
                recv_sem=recv_sem.at[stage],
                device_id=near_id(other),
                device_id_type=MESH,
            ).start()
            return carry

        lax.fori_loop(1, NEAR, go, 0)

    def all_of(stage, part):
        return pltpu.make_async_remote_copy(
            src_ref=part,
            dst_ref=part,
            send_sem=send_sem.at[stage],
            recv_sem=recv_sem.at[stage],
            device_id=near_id(near(1)),
            device_id_type=MESH,
        )

    far_waits = {
        X_FAR: x_far,
        Q_FAR: q_far,
        PART_FAR: sum_all,
        X_NEAR: x_all.at[pl.ds(0, NEAR - 1)],
        Q_NEAR: q_all.at[pl.ds(0, NEAR - 1)],
        PART_NEAR: part_all.at[pl.ds(0, NEAR - 1)],
        OUT_NEAR: att_all.at[pl.ds(0, NEAR - 1)],
    }

    def arrived(stage):
        all_of(stage, far_waits[stage]).wait_recv()

    pl.semaphore_wait(barrier, NEAR - 1 + 2 * BLOCKS)

    start_far(X_FAR, after, x_send, x_far)
    arrived(X_FAR)
    for u in range(2):
        tile = jnp.where(low, x_far[2 * u].astype(F32), x_far[2 * u + 1].astype(F32))
        x_pack[u] = tile.astype(BF16)
    x_all[mine] = x_pack[...]
    start_near(X_NEAR, lambda other: x_pack, x_all)
    arrived(X_NEAR)

    tiles = [None] * 32
    square = jnp.zeros((ROWS, HEAD), F32)
    for j in range(NEAR // 2):
        for u in range(2):
            even = x_all[2 * j, u].astype(F32)
            odd = x_all[2 * j + 1, u].astype(F32)
            square = square + even * even + odd * odd
            tiles[16 * u + j] = jnp.where(low, even, pltpu.roll(odd, 64, 1))
            tiles[16 * u + 8 + j] = jnp.where(low, pltpu.roll(even, 64, 1), odd)
    mean = jnp.sum(square, axis=1, keepdims=True) * (1.0 / 4096)
    shrink = lax.rsqrt(mean + 1e-05)
    normed = jnp.concatenate(
        [
            (tiles[t] * shrink * gain[:, HEAD * t : HEAD * (t + 1)]).astype(BF16)
            for t in range(32)
        ],
        axis=1,
    )
    columns = nt(normed, wq[...])
    place = tp % 4
    turned = columns
    for k in range(1, 4):
        turned = jnp.where(place == k, pltpu.roll(columns, 96 * k % 128, 1), turned)
    q_send[...] = turned.astype(BF16)

    start_far(Q_FAR, before, q_send, q_far)
    arrived(Q_FAR)
    q_all[mine] = q_far[...]
    start_near(Q_NEAR, lambda other: q_far, q_all)
    arrived(Q_NEAR)

    cosine, sine = turn[0], turn[1]
    for c in range(BLOCKS):
        for plane in range(4):
            b = [q_all[4 * plane + p, c].astype(F32) for p in range(4)]
            for k, edge in enumerate((96, 64, 32)):
                h = 3 * (4 * c + plane) + k
                head = jnp.where(lane < edge, b[k], b[k + 1])
                if h < QUERY_HEADS + KEY_HEADS:
                    head = head * cosine + pltpu.roll(head, 64, 1) * sine
                    head = head.astype(BF16).astype(F32)
                heads[h] = head

    hidden = jnp.concatenate([bias[...]] * 4, axis=0)
    for g in range(KEY_HEADS):
        cols = slice(g * HEAD, (g + 1) * HEAD)
        query = jnp.concatenate([heads[4 * g + k] for k in range(4)], axis=0).astype(BF16)
        score = nt(query, keys[:, cols]) * SCALE + hidden
        top = jnp.maximum(jnp.max(score, axis=1, keepdims=True), LOWEST)
        weight = jnp.exp(score - top)
        total = jnp.sum(weight, axis=1, keepdims=True)
        weighted = jnp.dot(
            weight.astype(BF16), values[:, cols], preferred_element_type=F32
        ).astype(BF16)
        stats = pack_stats(top, total, (4 * ROWS, HEAD))
        for k in range(2):
            part_send[2 * g + k, 0] = weighted[16 * k : 16 * (k + 1)]
            part_send[2 * g + k, 1] = stats[16 * k : 16 * (k + 1)]

    start_near(PART_NEAR, lambda other: part_send.at[other], part_all)
    part_all[mine] = part_send[mine]
    own_query = jnp.concatenate([heads[2 * mine], heads[2 * mine + 1]], axis=0)
    own_key = heads[QUERY_HEADS + mine // 2]
    own_value = heads[QUERY_HEADS + KEY_HEADS + mine // 2]
    own_score = (
        jnp.sum(own_query * jnp.concatenate([own_key] * 2, axis=0), axis=1, keepdims=True) * SCALE
    )
    own_score = jnp.where(block == 0, own_score, MASKED)
    arrived(PART_NEAR)
    stats = [unpack_stats(part_all[i, 1]) for i in range(NEAR)]
    top, total, weighted = merge(
        [s[0] for s in stats] + [own_score],
        [s[1] for s in stats] + [jnp.ones_like(own_score)],
        [part_all[i, 0].astype(F32) for i in range(NEAR)]
        + [jnp.concatenate([own_value] * 2, axis=0)],
    )
    sum_send[0] = weighted.astype(BF16)
    sum_send[1] = pack_stats(top, total, (2 * ROWS, HEAD))

    start_far(PART_FAR, after, sum_send, sum_all)
    arrived(PART_FAR)
    stats = [unpack_stats(sum_all[c, 1]) for c in range(BLOCKS)]
    top, total, weighted = merge(
        [s[0] for s in stats],
        [s[1] for s in stats],
        [sum_all[c, 0].astype(F32) for c in range(BLOCKS)],
    )
    att_send[...] = (weighted / total).astype(BF16)
    att_all[mine] = att_send[...]
    start_near(OUT_NEAR, lambda other: att_send, att_all)
    arrived(OUT_NEAR)
    pieces = []
    for i in range(NEAR):
        pair = att_all[i].astype(F32)
        pieces += [pair[:ROWS], pair[ROWS:]]
    attended = jnp.concatenate(pieces, axis=1).astype(BF16)
    out_ref[...] = nt(attended, wo[...]) + x_far[block].astype(F32)[:, :64]

    for stage, part in far_waits.items():
        all_of(stage, part).wait_send()


def local(x, gain, wq, wo, key_codes, value_codes, scale_table, owner, number, lengths, rows):
    half = HEAD // 2
    freq = ROPE_BASE ** (-np.arange(half, dtype=np.float64) / half)
    freq = jnp.asarray(np.concatenate([freq, freq]).astype(np.float32)[None, :])
    operands = (
        x[0],
        gain,
        jnp.swapaxes(wq[0], 0, 1),
        jnp.swapaxes(wo[0], 0, 1),
        key_codes[0].reshape(TOKENS, KEY_HEADS * HEAD),
        value_codes[0].reshape(TOKENS, KEY_HEADS * HEAD),
        scale_table[0],
        owner,
        number,
        lengths,
        rows,
        freq,
    )
    vmem, smem = pltpu.VMEM, pltpu.SMEM
    out = pl.pallas_call(
        kernel,
        out_shape=jax.ShapeDtypeStruct((ROWS, 64), F32),
        in_specs=[pl.BlockSpec(memory_space=pl.ANY)] * len(operands),
        out_specs=pl.BlockSpec(memory_space=pltpu.VMEM),
        scratch_shapes=[
            vmem((ROWS, 64), BF16),
            vmem((1, 4096), F32),
            vmem((128, 4096), BF16),
            vmem((64, 4096), BF16),
            vmem((TOKENS, 1024), BF16),
            vmem((TOKENS, 1024), BF16),
            vmem((SLOTS, 2, KEY_HEADS), F32),
            smem((1, SLOTS), I32),
            smem((1, SLOTS), I32),
            smem((1, 16), I32),
            smem((1, ROWS), I32),
            vmem((1, HEAD), F32),
            vmem((ROWS, TOKENS), F32),
            vmem((2, ROWS, HEAD), F32),
            vmem((ROWS, HEAD), BF16),
            vmem((BLOCKS, ROWS, HEAD), BF16),
            vmem((2, ROWS, HEAD), BF16),
            vmem((NEAR, 2, ROWS, HEAD), BF16),
            vmem((ROWS, HEAD), BF16),
            vmem((BLOCKS, ROWS, HEAD), BF16),
            vmem((NEAR, BLOCKS, ROWS, HEAD), BF16),
            vmem((HEADS, ROWS, HEAD), F32),
            vmem((NEAR, 2, 2 * ROWS, HEAD), BF16),
            vmem((NEAR, 2, 2 * ROWS, HEAD), BF16),
            vmem((2, 2 * ROWS, HEAD), BF16),
            vmem((BLOCKS, 2, 2 * ROWS, HEAD), BF16),
            vmem((2 * ROWS, HEAD), BF16),
            vmem((NEAR, 2 * ROWS, HEAD), BF16),
            pltpu.SemaphoreType.DMA((12,)),
            pltpu.SemaphoreType.DMA((7,)),
            pltpu.SemaphoreType.DMA((7,)),
        ],
        compiler_params=pltpu.CompilerParams(
            collective_id=0, has_side_effects=True, vmem_limit_bytes=32 * 2**20
        ),
    )(*operands)
    return out[None]


def solution(mesh):
    in_specs = (
        P("section", None, "tp"),
        P("section", None),
        P("section", None, "tp"),
        P("section", None, "tp"),
        P("section", "tp", None, None),
        P("section", "tp", None, None),
        P("section", "tp", None, None),
        P("section", "tp"),
        P("section", "tp"),
        P("section", None),
        P("section", None),
    )
    out_specs = P("section", None, "tp")
    return jax.shard_map(local, mesh=mesh, in_specs=in_specs, out_specs=out_specs, check_vma=False)
```

```python
import functools

import jax
import jax.numpy as jnp
import numpy as np
from jax import lax
from jax.experimental import pallas as pl
from jax.experimental.pallas import tpu as pltpu
from jax.sharding import PartitionSpec as P

MESH = pl.DeviceIdType.MESH
F32, BF16, I32 = jnp.float32, jnp.bfloat16, jnp.int32

ROWS = 8
HEAD = 128
QUERY_HEADS = 32
KEY_HEADS = 8
HEADS = QUERY_HEADS + 2 * KEY_HEADS
PAGE = 64
BLOCKS = 4
PLANES = 16
NEAR = 16
SLOTS = 8
TOKENS = SLOTS * PAGE
SCALE = 1.0 / HEAD**0.5
MASKED = -1e30
LOWEST = -1e25
ROPE_BASE = 500000.0
FARTHEST_FIRST = (7, 5, 3, 6, 1, 4, 2, 0)
TOGETHER = 2
X_LINE, X_PLANE, Q_LINE, Q_PLANE, PART_NEAR, PART_FAR, OUT_NEAR = range(7)


def nt(left, right):
    return lax.dot_general(
        left, right, (((1,), (1,)), ((), ())), preferred_element_type=F32
    )


def thirds(value):
    first = value.astype(BF16).astype(F32)
    rest = value - first
    second = rest.astype(BF16).astype(F32)
    return first, second, rest - second


def pack_stats(top, total, low, lane):
    slot = lane % (HEAD // 2) // 8
    pieces = thirds(top) + thirds(total)
    tiles = []
    for at in range(0, top.shape[0], 2 * ROWS):
        tile = jnp.zeros(lane.shape, F32)
        for k, piece in enumerate(pieces):
            pair = jnp.where(low, piece[at : at + ROWS], piece[at + ROWS : at + 2 * ROWS])
            tile = jnp.where(slot == k, pair, tile)
        tiles.append(tile.astype(BF16))
    return tiles


def unpack_stats(tile):
    wide = tile.astype(F32)
    part = [
        jnp.concatenate([wide[:, at : at + 1], wide[:, at + 64 : at + 65]], axis=0)
        for at in range(0, 48, 8)
    ]
    return part[0] + part[1] + part[2], part[3] + part[4] + part[5]


def both(parts):
    return jnp.concatenate([parts[0].astype(F32), parts[1].astype(F32)], axis=0)


def merge(tops, totals, sums):
    top = functools.reduce(jnp.maximum, tops)
    total, weighted = 0.0, 0.0
    for t, l, a in zip(tops, totals, sums):
        factor = jnp.exp(t - top)
        total = total + factor * l
        weighted = weighted + factor * a
    return top, total, weighted


def kernel(
    x_hbm,
    gain_hbm,
    wq_hbm,
    wo_hbm,
    key_hbm,
    value_hbm,
    scale_hbm,
    owner_hbm,
    number_hbm,
    length_hbm,
    row_hbm,
    freq_hbm,
    out_ref,
    x_own,
    gain,
    wq,
    wo,
    keys,
    values,
    scales,
    owner,
    number,
    length,
    row,
    freq,
    bias,
    turn,
    x_send,
    x_line,
    x_pack,
    x_all,
    q_send,
    q_line,
    q_all,
    heads,
    part_send,
    part_all,
    sum_send,
    sum_all,
    att_send,
    att_all,
    local_sem,
    send_sem,
    recv_sem,
):
    section = lax.axis_index("section")
    tp = lax.axis_index("tp")
    block, mine = tp // NEAR, tp % NEAR
    plane, place = tp // 4, tp % 4
    sections = lax.axis_size("section")
    after = lax.rem(section + 1, sections)
    before = lax.rem(section + sections - 1, sections)

    def near(d):
        return lax.rem(mine + d, NEAR)

    def near_id(other):
        return {"tp": block * NEAR + other}

    def far_id(where, other):
        return {"section": where, "tp": other * NEAR + mine}

    def line_id(other):
        return {"tp": other * 4 + place}

    def plane_id(where, other):
        return {"section": where, "tp": plane * 4 + other}

    barrier = pltpu.get_barrier_semaphore()

    def greet(device):
        pl.semaphore_signal(barrier, inc=1, device_id=device, device_id_type=MESH)

    def greet_line(k, carry):
        greet(line_id(lax.rem(plane + k, PLANES)))
        return carry

    def greet_shift(k, carry):
        for where in (before, after):
            greet(plane_id(where, k))
        return carry

    def greet_far(k, carry):
        other = lax.rem(block + k, BLOCKS)
        for where in (before, after):
            greet(far_id(where, other))
        return carry

    def greet_near(k, carry):
        @pl.when(lax.rem(mine + k, 4) != place)
        def _():
            greet(near_id(near(k)))

        return carry

    lax.fori_loop(1, PLANES, greet_line, 0)
    lax.fori_loop(0, 4, greet_shift, 0)
    lax.fori_loop(1, BLOCKS, greet_far, 0)
    lax.fori_loop(1, NEAR, greet_near, 0)
    greetings = PLANES - 1 + 8 + 2 * (BLOCKS - 1) + NEAR - 4

    moves = [
        pltpu.make_async_copy(src, dst, local_sem.at[k])
        for k, (src, dst) in enumerate(
            [
                (x_hbm, x_own),
                (row_hbm, row),
                (length_hbm, length),
                (owner_hbm, owner),
                (number_hbm, number),
                (scale_hbm, scales),
                (freq_hbm, freq),
                (key_hbm, keys),
                (value_hbm, values),
                (gain_hbm, gain),
                (wq_hbm, wq.at[pl.ds(0, 96)]),
                (wo_hbm, wo),
            ]
        )
    ]
    for move in moves:
        move.start()
    wq[96:128, :] = jnp.zeros((32, wq.shape[1]), BF16)

    moves[0].wait()
    x_here = x_own[...].astype(F32)
    x_send[...] = jnp.concatenate([x_here, x_here], axis=1).astype(BF16)

    lane = lax.broadcasted_iota(I32, (ROWS, HEAD), 1)
    low = lane < HEAD // 2

    def prepare():
        for k in range(1, 7):
            moves[k].wait()
        sub = lax.broadcasted_iota(I32, (ROWS, HEAD), 0)
        row_of = jnp.zeros((ROWS, HEAD), I32)
        limit = jnp.zeros((ROWS, HEAD), I32)
        for r in range(ROWS):
            request = row[0, r]
            row_of = jnp.where(sub == r, request, row_of)
            limit = jnp.where(sub == r, length[0, request], limit)
        for j in range(SLOTS // 2):
            tok_owner = jnp.where(low, owner[0, 2 * j], owner[0, 2 * j + 1])
            tok_page = jnp.where(low, number[0, 2 * j], number[0, 2 * j + 1])
            tok_pos = tok_page * PAGE + lane % PAGE
            seen = (tok_owner == row_of) & (tok_pos < limit)
            bias[:, HEAD * j : HEAD * (j + 1)] = jnp.where(seen, 0.0, MASKED)
        angle = limit.astype(F32) * freq[...]
        turn[0] = jnp.cos(angle)
        sine = jnp.sin(angle)
        turn[1] = jnp.where(low, -sine, sine)

        moves[7].wait()
        moves[8].wait()

        def restore(k, carry):
            at = pl.ds(pl.multiple_of(k * PAGE, PAGE), PAGE)
            both = scales[k]
            for which, store in ((0, keys), (1, values)):
                for g in range(KEY_HEADS):
                    cols = pl.ds(g * HEAD, HEAD)
                    factor = jnp.broadcast_to(both[which : which + 1, g : g + 1], (PAGE, HEAD))
                    store[at, cols] = (store[at, cols].astype(F32) * factor).astype(BF16)
            return carry

        lax.fori_loop(0, SLOTS, restore, 0)
        moves[9].wait()
        moves[10].wait()
        moves[11].wait()

    def send(stage, src, dst, device):
        pltpu.make_async_remote_copy(
            src_ref=src,
            dst_ref=dst,
            send_sem=send_sem.at[stage],
            recv_sem=recv_sem.at[stage],
            device_id=device,
            device_id_type=MESH,
        ).start()

    def start_far(stage, where, src, dst):
        def go(d, carry):
            other = lax.rem(block + BLOCKS // 2 + d, BLOCKS)
            send(stage, src, dst.at[block], far_id(where, other))
            return carry

        lax.fori_loop(0, BLOCKS, go, 0)

    def start_near(stage, src, dst):
        def go(d, carry):
            send(stage, src, dst.at[mine], near_id(near(d)))
            return carry

        lax.fori_loop(1, NEAR, go, 0)

    def start_line(stage, src, dst):
        half = PLANES // 2
        send(stage, src, dst.at[plane], line_id(lax.rem(plane + half, PLANES)))

        def go(d, carry):
            for shift in (half - d, half + d):
                send(stage, src, dst.at[plane], line_id(lax.rem(plane + shift, PLANES)))
            return carry

        lax.fori_loop(1, half, go, 0)

    def start_plane(stage, where, src, dst):
        def go(d, carry):
            send(stage, src, dst.at[place], plane_id(where, lax.rem(place + 3 - d, 4)))
            return carry

        lax.fori_loop(0, 4, go, 0)

    def all_of(stage, part):
        return pltpu.make_async_remote_copy(
            src_ref=part,
            dst_ref=part,
            send_sem=send_sem.at[stage],
            recv_sem=recv_sem.at[stage],
            device_id=near_id(near(1)),
            device_id_type=MESH,
        )

    expected = {
        X_LINE: x_line.at[pl.ds(0, PLANES - 1)],
        X_PLANE: x_all,
        Q_LINE: q_line.at[pl.ds(0, PLANES - 1)],
        Q_PLANE: q_all,
        PART_NEAR: part_all.at[pl.ds(0, NEAR - 1)],
        PART_FAR: sum_all,
        OUT_NEAR: att_all.at[pl.ds(0, NEAR - 1)],
    }

    def arrived(stage):
        all_of(stage, expected[stage]).wait_recv()

    early = plane < PLANES // 2
    pl.when(early)(prepare)
    pl.semaphore_wait(barrier, greetings)

    start_line(X_LINE, x_send, x_line)
    x_line[plane] = x_send[...]
    pl.when(jnp.logical_not(early))(prepare)
    arrived(X_LINE)
    for u in range(PLANES // 2):
        tile = jnp.where(low, x_line[2 * u].astype(F32), x_line[2 * u + 1].astype(F32))
        x_pack[u] = tile.astype(BF16)
    start_plane(X_PLANE, after, x_pack, x_all)
    arrived(X_PLANE)

    tiles = [None] * 32
    square = jnp.zeros((ROWS, HEAD), F32)
    for u in range(PLANES // 2):
        for j in range(2):
            even = x_all[2 * j, u].astype(F32)
            odd = x_all[2 * j + 1, u].astype(F32)
            square = square + even * even + odd * odd
            tiles[4 * u + j] = jnp.where(low, even, pltpu.roll(odd, 64, 1))
            tiles[4 * u + 2 + j] = jnp.where(low, pltpu.roll(even, 64, 1), odd)
    mean = jnp.sum(square, axis=1, keepdims=True) * (1.0 / 4096)
    shrink = lax.rsqrt(mean + 1e-05)
    normed = jnp.concatenate(
        [
            (tiles[t] * shrink * gain[:, HEAD * t : HEAD * (t + 1)]).astype(BF16)
            for t in range(32)
        ],
        axis=1,
    )
    columns = nt(normed, wq[...])
    turned = columns
    for k in range(1, 4):
        turned = jnp.where(place == k, pltpu.roll(columns, 96 * k % 128, 1), turned)
    q_send[...] = turned.astype(BF16)

    start_line(Q_LINE, q_send, q_line)
    q_line[plane] = q_send[...]
    arrived(Q_LINE)
    start_plane(Q_PLANE, before, q_line, q_all)
    arrived(Q_PLANE)

    cosine, sine = turn[0], turn[1]
    for z in range(PLANES):
        b = [q_all[p, z].astype(F32) for p in range(4)]
        for k, edge in enumerate((96, 64, 32)):
            head = jnp.where(lane < edge, b[k], b[k + 1])
            if 3 * z + k < QUERY_HEADS + KEY_HEADS:
                head = head * cosine + pltpu.roll(head, 64, 1) * sine
                head = head.astype(BF16).astype(F32)
            heads[3 * z + k] = head

    hidden = jnp.concatenate([bias[...]] * 4, axis=0)
    chip = mine // 2
    for at in range(0, len(FARTHEST_FIRST), TOGETHER):
        steps = FARTHEST_FIRST[at : at + TOGETHER]
        groups = [chip ^ k for k in steps]
        cols = [pl.ds(pl.multiple_of(g * HEAD, HEAD), HEAD) for g in groups]
        queries = [heads[pl.ds(4 * g, 4)].reshape(4 * ROWS, HEAD).astype(BF16) for g in groups]
        scores = [nt(q, keys[:, c]) * SCALE + hidden for q, c in zip(queries, cols)]
        tops = [jnp.maximum(jnp.max(s, axis=1, keepdims=True), LOWEST) for s in scores]
        weights = [jnp.exp(s - t) for s, t in zip(scores, tops)]
        sums = [
            jnp.dot(w.astype(BF16), values[:, c], preferred_element_type=F32).astype(BF16)
            for w, c in zip(weights, cols)
        ]
        totals = [jnp.sum(w, axis=1, keepdims=True) for w in weights]
        for n, g in enumerate(groups):
            first, second = pack_stats(tops[n], totals[n], low, lane)
            for core, stats in ((0, first), (1, second)):
                part_send[2 * g + core, 0] = sums[n][16 * core : 16 * core + 8]
                part_send[2 * g + core, 1] = sums[n][16 * core + 8 : 16 * core + 16]
                part_send[2 * g + core, 2] = stats
        for k, g in zip(steps, groups):
            if k:
                for other in (2 * g, 2 * g + 1):
                    send(PART_NEAR, part_send.at[other], part_all.at[mine], near_id(other))
    sibling = mine + 1 - 2 * (mine % 2)
    send(PART_NEAR, part_send.at[sibling], part_all.at[mine], near_id(sibling))
    part_all[mine] = part_send[mine]
    own_query = jnp.concatenate([heads[2 * mine], heads[2 * mine + 1]], axis=0)
    own_key = heads[QUERY_HEADS + mine // 2]
    own_value = heads[QUERY_HEADS + KEY_HEADS + mine // 2]
    own_score = (
        jnp.sum(own_query * jnp.concatenate([own_key] * 2, axis=0), axis=1, keepdims=True) * SCALE
    )
    own_score = jnp.where(block == 0, own_score, MASKED)
    arrived(PART_NEAR)
    stats = [unpack_stats(part_all[i, 2]) for i in range(NEAR)]
    top, total, weighted = merge(
        [s[0] for s in stats] + [own_score],
        [s[1] for s in stats] + [jnp.ones_like(own_score)],
        [both(part_all[i]) for i in range(NEAR)]
        + [jnp.concatenate([own_value] * 2, axis=0)],
    )
    sum_send[0] = weighted[:ROWS].astype(BF16)
    sum_send[1] = weighted[ROWS:].astype(BF16)
    sum_send[2] = pack_stats(top, total, low, lane)[0]

    start_far(PART_FAR, after, sum_send, sum_all)
    arrived(PART_FAR)
    stats = [unpack_stats(sum_all[c, 2]) for c in range(BLOCKS)]
    top, total, weighted = merge(
        [s[0] for s in stats],
        [s[1] for s in stats],
        [both(sum_all[c]) for c in range(BLOCKS)],
    )
    att_send[...] = (weighted / total).astype(BF16)
    att_all[mine] = att_send[...]
    start_near(OUT_NEAR, att_send, att_all)
    arrived(OUT_NEAR)
    pieces = []
    for i in range(NEAR):
        pair = att_all[i].astype(F32)
        pieces += [pair[:ROWS], pair[ROWS:]]
    attended = jnp.concatenate(pieces, axis=1).astype(BF16)
    x_here = x_all[place, plane // 2].astype(F32)
    x_here = jnp.where(plane % 2 == 0, x_here, pltpu.roll(x_here, 64, 1))[:, :64]
    out_ref[...] = nt(attended, wo[...]) + x_here

    for stage, part in expected.items():
        all_of(stage, part).wait_send()


def local(x, gain, wq, wo, key_codes, value_codes, scale_table, owner, number, lengths, rows):
    half = HEAD // 2
    freq = ROPE_BASE ** (-np.arange(half, dtype=np.float64) / half)
    freq = jnp.asarray(np.concatenate([freq, freq]).astype(np.float32)[None, :])
    operands = (
        x[0],
        gain,
        jnp.swapaxes(wq[0], 0, 1),
        jnp.swapaxes(wo[0], 0, 1),
        key_codes[0].reshape(TOKENS, KEY_HEADS * HEAD),
        value_codes[0].reshape(TOKENS, KEY_HEADS * HEAD),
        scale_table[0],
        owner,
        number,
        lengths,
        rows,
        freq,
    )
    vmem, smem = pltpu.VMEM, pltpu.SMEM
    out = pl.pallas_call(
        kernel,
        out_shape=jax.ShapeDtypeStruct((ROWS, 64), F32),
        in_specs=[pl.BlockSpec(memory_space=pltpu.HBM)] * len(operands),
        out_specs=pl.BlockSpec(memory_space=pltpu.VMEM),
        scratch_shapes=[
            vmem((ROWS, 64), BF16),
            vmem((1, 4096), F32),
            vmem((128, 4096), BF16),
            vmem((64, 4096), BF16),
            vmem((TOKENS, 1024), BF16),
            vmem((TOKENS, 1024), BF16),
            vmem((SLOTS, 2, KEY_HEADS), F32),
            smem((1, SLOTS), I32),
            smem((1, SLOTS), I32),
            smem((1, 16), I32),
            smem((1, ROWS), I32),
            vmem((1, HEAD), F32),
            vmem((ROWS, TOKENS), F32),
            vmem((2, ROWS, HEAD), F32),
            vmem((ROWS, HEAD), BF16),
            vmem((PLANES, ROWS, HEAD), BF16),
            vmem((PLANES // 2, ROWS, HEAD), BF16),
            vmem((4, PLANES // 2, ROWS, HEAD), BF16),
            vmem((ROWS, HEAD), BF16),
            vmem((PLANES, ROWS, HEAD), BF16),
            vmem((4, PLANES, ROWS, HEAD), BF16),
            vmem((HEADS, ROWS, HEAD), F32),
            vmem((NEAR, 3, ROWS, HEAD), BF16),
            vmem((NEAR, 3, ROWS, HEAD), BF16),
            vmem((3, ROWS, HEAD), BF16),
            vmem((BLOCKS, 3, ROWS, HEAD), BF16),
            vmem((2 * ROWS, HEAD), BF16),
            vmem((NEAR, 2 * ROWS, HEAD), BF16),
            pltpu.SemaphoreType.DMA((12,)),
            pltpu.SemaphoreType.DMA((7,)),
            pltpu.SemaphoreType.DMA((7,)),
        ],
        compiler_params=pltpu.CompilerParams(
            collective_id=0, has_side_effects=True, vmem_limit_bytes=60 * 2**20
        ),
    )(*operands)
    return out[None]


def solution(mesh):
    in_specs = (
        P("section", None, "tp"),
        P("section", None),
        P("section", None, "tp"),
        P("section", None, "tp"),
        P("section", "tp", None, None),
        P("section", "tp", None, None),
        P("section", "tp", None, None),
        P("section", "tp"),
        P("section", "tp"),
        P("section", None),
        P("section", None),
    )
    out_specs = P("section", None, "tp")
    return jax.shard_map(local, mesh=mesh, in_specs=in_specs, out_specs=out_specs, check_vma=False)
```

```python
import functools

import jax
import jax.numpy as jnp
import numpy as np
from jax import lax
from jax.experimental import pallas as pl
from jax.experimental.pallas import tpu as pltpu
from jax.sharding import PartitionSpec as P

MESH = pl.DeviceIdType.MESH
F32, BF16, I32 = jnp.float32, jnp.bfloat16, jnp.int32

ROWS = 8
HEAD = 128
QUERY_HEADS = 32
KEY_HEADS = 8
HEADS = QUERY_HEADS + 2 * KEY_HEADS
PAGE = 64
BLOCKS = 4
PLANES = 16
NEAR = 16
SLOTS = 8
TOKENS = SLOTS * PAGE
SCALE = 1.0 / HEAD**0.5
MASKED = -1e30
LOWEST = -1e25
ROPE_BASE = 500000.0
LINE_ORDER = (8, 7, 9, 6, 10, 5, 11, 4, 12, 3, 13, 2, 14, 1, 15)
FARTHEST_FIRST = (7, 5, 3, 6, 1, 4, 2, 0)
SHIFTED_FARTHEST_FIRST = (7, 6, 5, 4, 3, 2, 1, 0)
TOGETHER = 2
X_LINE, X_PLANE, Q_LINE, Q_PLANE, PART_NEAR, PART_FAR, OUT_NEAR = range(7)


def nt(left, right):
    return lax.dot_general(
        left, right, (((1,), (1,)), ((), ())), preferred_element_type=F32
    )


def thirds(value):
    first = value.astype(BF16).astype(F32)
    rest = value - first
    second = rest.astype(BF16).astype(F32)
    return first, second, rest - second


def pack_stats(top, total, low, lane):
    slot = lane % (HEAD // 2) // 8
    pieces = thirds(top) + thirds(total)
    tiles = []
    for at in range(0, top.shape[0], 2 * ROWS):
        tile = jnp.zeros(lane.shape, F32)
        for k, piece in enumerate(pieces):
            pair = jnp.where(low, piece[at : at + ROWS], piece[at + ROWS : at + 2 * ROWS])
            tile = jnp.where(slot == k, pair, tile)
        tiles.append(tile.astype(BF16))
    return tiles


def unpack_stats(tile):
    wide = tile.astype(F32)
    part = [
        jnp.concatenate([wide[:, at : at + 1], wide[:, at + 64 : at + 65]], axis=0)
        for at in range(0, 48, 8)
    ]
    return part[0] + part[1] + part[2], part[3] + part[4] + part[5]


def both(parts):
    return jnp.concatenate([parts[0].astype(F32), parts[1].astype(F32)], axis=0)


def merge(tops, totals, sums):
    top = functools.reduce(jnp.maximum, tops)
    total, weighted = 0.0, 0.0
    for t, l, a in zip(tops, totals, sums):
        factor = jnp.exp(t - top)
        total = total + factor * l
        weighted = weighted + factor * a
    return top, total, weighted


def kernel(
    x_hbm,
    gain_hbm,
    wq_hbm,
    wo_hbm,
    key_hbm,
    value_hbm,
    scale_hbm,
    owner_hbm,
    number_hbm,
    length_hbm,
    row_hbm,
    freq_hbm,
    out_ref,
    x_own,
    gain,
    wq,
    wo,
    keys,
    values,
    scales,
    owner,
    number,
    length,
    row,
    freq,
    bias,
    turn,
    x_send,
    x_line,
    x_pack,
    x_all,
    q_send,
    q_line,
    q_all,
    heads,
    part_send,
    part_all,
    sum_send,
    sum_all,
    att_send,
    att_all,
    local_sem,
    send_sem,
    recv_sem,
):
    section = lax.axis_index("section")
    tp = lax.axis_index("tp")
    block, mine = tp // NEAR, tp % NEAR
    plane, place = tp // 4, tp % 4
    sections = lax.axis_size("section")
    after = lax.rem(section + 1, sections)
    before = lax.rem(section + sections - 1, sections)

    def near_id(other):
        return {"tp": block * NEAR + other}

    def far_id(other):
        return {"tp": other * NEAR + mine}

    def shifted_near_id(other):
        return {"section": after, "tp": block * NEAR + other}

    def line_id(other):
        return {"tp": other * 4 + place}

    def plane_id(where, other):
        return {"section": where, "tp": plane * 4 + other}

    barrier = pltpu.get_barrier_semaphore()

    def greet(device):
        pl.semaphore_signal(barrier, inc=1, device_id=device, device_id_type=MESH)

    for k in LINE_ORDER:
        greet(line_id(lax.rem(plane + k, PLANES)))
    for k in range(4):
        greet(plane_id(before, k))
    greetings = PLANES - 1 + 4

    moves = [
        pltpu.make_async_copy(src, dst, local_sem.at[k])
        for k, (src, dst) in enumerate(
            [
                (x_hbm, x_own),
                (row_hbm, row),
                (length_hbm, length),
                (owner_hbm, owner),
                (number_hbm, number),
                (scale_hbm, scales),
                (freq_hbm, freq),
                (key_hbm, keys),
                (value_hbm, values),
                (gain_hbm, gain),
                (wq_hbm, wq.at[pl.ds(0, 96)]),
                (wo_hbm, wo),
            ]
        )
    ]
    for move in moves:
        move.start()
    wq[96:128, :] = jnp.zeros((32, wq.shape[1]), BF16)

    moves[0].wait()
    x_here = x_own[...].astype(F32)
    x_send[...] = jnp.concatenate([x_here, x_here], axis=1).astype(BF16)

    lane = lax.broadcasted_iota(I32, (ROWS, HEAD), 1)
    low = lane < HEAD // 2

    def prepare():
        for k in range(1, 7):
            moves[k].wait()
        sub = lax.broadcasted_iota(I32, (ROWS, HEAD), 0)
        row_of = jnp.zeros((ROWS, HEAD), I32)
        limit = jnp.zeros((ROWS, HEAD), I32)
        for r in range(ROWS):
            request = row[0, r]
            row_of = jnp.where(sub == r, request, row_of)
            limit = jnp.where(sub == r, length[0, request], limit)
        for j in range(SLOTS // 2):
            tok_owner = jnp.where(low, owner[0, 2 * j], owner[0, 2 * j + 1])
            tok_page = jnp.where(low, number[0, 2 * j], number[0, 2 * j + 1])
            tok_pos = tok_page * PAGE + lane % PAGE
            seen = (tok_owner == row_of) & (tok_pos < limit)
            bias[:, HEAD * j : HEAD * (j + 1)] = jnp.where(seen, 0.0, MASKED)
        angle = limit.astype(F32) * freq[...]
        turn[0] = jnp.cos(angle)
        sine = jnp.sin(angle)
        turn[1] = jnp.where(low, -sine, sine)

        moves[7].wait()
        moves[8].wait()

        def restore(k, carry):
            at = pl.ds(pl.multiple_of(k * PAGE, PAGE), PAGE)
            both = scales[k]
            for which, store in ((0, keys), (1, values)):
                for g in range(KEY_HEADS):
                    cols = pl.ds(g * HEAD, HEAD)
                    factor = jnp.broadcast_to(both[which : which + 1, g : g + 1], (PAGE, HEAD))
                    store[at, cols] = (store[at, cols].astype(F32) * factor).astype(BF16)
            return carry

        lax.fori_loop(0, SLOTS, restore, 0)
        moves[9].wait()
        moves[10].wait()
        moves[11].wait()

    def send(stage, src, dst, device):
        pltpu.make_async_remote_copy(
            src_ref=src,
            dst_ref=dst,
            send_sem=send_sem.at[stage],
            recv_sem=recv_sem.at[stage],
            device_id=device,
            device_id_type=MESH,
        ).start()

    def start_far(stage, src, dst):
        for shift in (2, 1, 3):
            send(stage, src, dst.at[block], far_id(lax.rem(block + shift, BLOCKS)))

    chip, core = mine // 2, mine % 2
    sibling = 2 * chip + 1 - core

    def start_near(stage, src, dst):
        for k in FARTHEST_FIRST[:-1]:
            for other in (0, 1):
                send(stage, src, dst.at[mine], near_id(2 * (chip ^ k) + other))
        send(stage, src, dst.at[mine], near_id(sibling))

    def start_line(stage, src, dst):
        for k in LINE_ORDER:
            send(stage, src, dst.at[plane], line_id(lax.rem(plane + k, PLANES)))

    def start_plane(stage, where, src, dst):
        for k in (3, 2, 1, 0):
            send(stage, src, dst.at[place], plane_id(where, place ^ k))

    def all_of(stage, part):
        return pltpu.make_async_remote_copy(
            src_ref=part,
            dst_ref=part,
            send_sem=send_sem.at[stage],
            recv_sem=recv_sem.at[stage],
            device_id=near_id(sibling),
            device_id_type=MESH,
        )

    expected = {
        X_LINE: x_line.at[pl.ds(0, PLANES - 1)],
        X_PLANE: x_all,
        Q_LINE: q_line.at[pl.ds(0, PLANES - 1)],
        Q_PLANE: q_all,
        PART_NEAR: part_all,
        PART_FAR: sum_all.at[pl.ds(0, BLOCKS - 1)],
        OUT_NEAR: att_all.at[pl.ds(0, NEAR - 1)],
    }

    def arrived(stage):
        all_of(stage, expected[stage]).wait_recv()

    early = plane < PLANES // 2
    pl.when(early)(prepare)
    pl.semaphore_wait(barrier, greetings)

    start_line(X_LINE, x_send, x_line)
    x_line[plane] = x_send[...]
    pl.when(jnp.logical_not(early))(prepare)
    arrived(X_LINE)
    for u in range(PLANES // 2):
        tile = jnp.where(low, x_line[2 * u].astype(F32), x_line[2 * u + 1].astype(F32))
        x_pack[u] = tile.astype(BF16)
    start_plane(X_PLANE, after, x_pack, x_all)
    arrived(X_PLANE)

    tiles = [None] * 32
    square = jnp.zeros((ROWS, HEAD), F32)
    for u in range(PLANES // 2):
        for j in range(2):
            even = x_all[2 * j, u].astype(F32)
            odd = x_all[2 * j + 1, u].astype(F32)
            square = square + even * even + odd * odd
            tiles[4 * u + j] = jnp.where(low, even, pltpu.roll(odd, 64, 1))
            tiles[4 * u + 2 + j] = jnp.where(low, pltpu.roll(even, 64, 1), odd)
    mean = jnp.sum(square, axis=1, keepdims=True) * (1.0 / 4096)
    shrink = lax.rsqrt(mean + 1e-05)
    normed = jnp.concatenate(
        [
            (tiles[t] * shrink * gain[:, HEAD * t : HEAD * (t + 1)]).astype(BF16)
            for t in range(32)
        ],
        axis=1,
    )
    columns = nt(normed, wq[...])
    turned = columns
    for k in range(1, 4):
        turned = jnp.where(place == k, pltpu.roll(columns, 96 * k % 128, 1), turned)
    q_send[...] = turned.astype(BF16)

    start_line(Q_LINE, q_send, q_line)
    q_line[plane] = q_send[...]
    arrived(Q_LINE)
    start_plane(Q_PLANE, before, q_line, q_all)
    arrived(Q_PLANE)

    cosine, sine = turn[0], turn[1]
    for z in range(PLANES):
        b = [q_all[p, z].astype(F32) for p in range(4)]
        for k, edge in enumerate((96, 64, 32)):
            head = jnp.where(lane < edge, b[k], b[k + 1])
            if 3 * z + k < QUERY_HEADS + KEY_HEADS:
                head = head * cosine + pltpu.roll(head, 64, 1) * sine
                head = head.astype(BF16).astype(F32)
            heads[3 * z + k] = head

    hidden = jnp.concatenate([bias[...]] * 4, axis=0)
    for at in range(0, KEY_HEADS, TOGETHER):
        steps = SHIFTED_FARTHEST_FIRST[at : at + TOGETHER]
        groups = [chip ^ k for k in steps]
        cols = [pl.ds(pl.multiple_of(g * HEAD, HEAD), HEAD) for g in groups]
        queries = [heads[pl.ds(4 * g, 4)].reshape(4 * ROWS, HEAD).astype(BF16) for g in groups]
        scores = [nt(q, keys[:, c]) * SCALE + hidden for q, c in zip(queries, cols)]
        tops = [jnp.maximum(jnp.max(s, axis=1, keepdims=True), LOWEST) for s in scores]
        weights = [jnp.exp(s - t) for s, t in zip(scores, tops)]
        sums = [
            jnp.dot(w.astype(BF16), values[:, c], preferred_element_type=F32)
            for w, c in zip(weights, cols)
        ]
        totals = [jnp.sum(w, axis=1, keepdims=True) for w in weights]
        if steps[-1] == 0:
            new_key = jnp.concatenate([heads[QUERY_HEADS + chip]] * 4, axis=0)
            new_value = jnp.concatenate([heads[QUERY_HEADS + KEY_HEADS + chip]] * 4, axis=0)
            own = jnp.sum(queries[-1].astype(F32) * new_key, axis=1, keepdims=True) * SCALE
            pair = lax.broadcasted_iota(I32, (4 * ROWS, 1), 0) // (2 * ROWS)
            own = jnp.where((pair == core) & (block == 0), own, MASKED)
            top = jnp.maximum(tops[-1], own)
            old_weight, own_weight = jnp.exp(tops[-1] - top), jnp.exp(own - top)
            totals[-1] = totals[-1] * old_weight + own_weight
            sums[-1] = sums[-1] * old_weight + own_weight * new_value
            tops[-1] = top
        sums = [s.astype(BF16) for s in sums]
        for n, g in enumerate(groups):
            first, second = pack_stats(tops[n], totals[n], low, lane)
            for c, stats in ((0, first), (1, second)):
                part_send[2 * g + c, 0] = sums[n][16 * c : 16 * c + 8]
                part_send[2 * g + c, 1] = sums[n][16 * c + 8 : 16 * c + 16]
                part_send[2 * g + c, 2] = stats
        for g in groups:
            for other in (2 * g, 2 * g + 1):
                send(PART_NEAR, part_send.at[other], part_all.at[mine], shifted_near_id(other))

    arrived(PART_NEAR)
    stats = [unpack_stats(part_all[i, 2]) for i in range(NEAR)]
    top, total, weighted = merge(
        [s[0] for s in stats],
        [s[1] for s in stats],
        [both(part_all[i]) for i in range(NEAR)],
    )
    sum_send[0] = weighted[:ROWS].astype(BF16)
    sum_send[1] = weighted[ROWS:].astype(BF16)
    sum_send[2] = pack_stats(top, total, low, lane)[0]

    start_far(PART_FAR, sum_send, sum_all)
    sum_all[block] = sum_send[...]
    arrived(PART_FAR)
    stats = [unpack_stats(sum_all[c, 2]) for c in range(BLOCKS)]
    top, total, weighted = merge(
        [s[0] for s in stats],
        [s[1] for s in stats],
        [both(sum_all[c]) for c in range(BLOCKS)],
    )
    att_send[...] = (weighted / total).astype(BF16)
    att_all[mine] = att_send[...]
    start_near(OUT_NEAR, att_send, att_all)
    arrived(OUT_NEAR)
    pieces = []
    for i in range(NEAR):
        pair = att_all[i].astype(F32)
        pieces += [pair[:ROWS], pair[ROWS:]]
    attended = jnp.concatenate(pieces, axis=1).astype(BF16)
    x_here = x_all[place, plane // 2].astype(F32)
    x_here = jnp.where(plane % 2 == 0, x_here, pltpu.roll(x_here, 64, 1))[:, :64]
    out_ref[...] = nt(attended, wo[...]) + x_here

    for stage, part in expected.items():
        all_of(stage, part).wait_send()


def local(x, gain, wq, wo, key_codes, value_codes, scale_table, owner, number, lengths, rows):
    half = HEAD // 2
    freq = ROPE_BASE ** (-np.arange(half, dtype=np.float64) / half)
    freq = jnp.asarray(np.concatenate([freq, freq]).astype(np.float32)[None, :])
    operands = (
        x[0],
        gain,
        jnp.swapaxes(wq[0], 0, 1),
        jnp.swapaxes(wo[0], 0, 1),
        key_codes[0].reshape(TOKENS, KEY_HEADS * HEAD),
        value_codes[0].reshape(TOKENS, KEY_HEADS * HEAD),
        scale_table[0],
        owner,
        number,
        lengths,
        rows,
        freq,
    )
    operands = [pltpu.with_memory_space_constraint(x, pltpu.HBM) for x in operands]
    vmem, smem = pltpu.VMEM, pltpu.SMEM
    out = pl.pallas_call(
        kernel,
        out_shape=vmem((ROWS, 64), F32),
        in_specs=[pl.BlockSpec(memory_space=pltpu.HBM)] * len(operands),
        out_specs=pl.BlockSpec(memory_space=pltpu.VMEM),
        scratch_shapes=[
            vmem((ROWS, 64), BF16),
            vmem((1, 4096), F32),
            vmem((128, 4096), BF16),
            vmem((64, 4096), BF16),
            vmem((TOKENS, 1024), BF16),
            vmem((TOKENS, 1024), BF16),
            vmem((SLOTS, 2, KEY_HEADS), F32),
            smem((1, SLOTS), I32),
            smem((1, SLOTS), I32),
            smem((1, 16), I32),
            smem((1, ROWS), I32),
            vmem((1, HEAD), F32),
            vmem((ROWS, TOKENS), F32),
            vmem((2, ROWS, HEAD), F32),
            vmem((ROWS, HEAD), BF16),
            vmem((PLANES, ROWS, HEAD), BF16),
            vmem((PLANES // 2, ROWS, HEAD), BF16),
            vmem((4, PLANES // 2, ROWS, HEAD), BF16),
            vmem((ROWS, HEAD), BF16),
            vmem((PLANES, ROWS, HEAD), BF16),
            vmem((4, PLANES, ROWS, HEAD), BF16),
            vmem((HEADS, ROWS, HEAD), F32),
            vmem((NEAR, 3, ROWS, HEAD), BF16),
            vmem((NEAR, 3, ROWS, HEAD), BF16),
            vmem((3, ROWS, HEAD), BF16),
            vmem((BLOCKS, 3, ROWS, HEAD), BF16),
            vmem((2 * ROWS, HEAD), BF16),
            vmem((NEAR, 2 * ROWS, HEAD), BF16),
            pltpu.SemaphoreType.DMA((12,)),
            pltpu.SemaphoreType.DMA((7,)),
            pltpu.SemaphoreType.DMA((7,)),
        ],
        compiler_params=pltpu.CompilerParams(
            collective_id=0, has_side_effects=True, vmem_limit_bytes=40 * 2**20
        ),
    )(*operands)
    return out[None]


def solution(mesh):
    in_specs = (
        P("section", None, "tp"),
        P("section", None),
        P("section", None, "tp"),
        P("section", None, "tp"),
        P("section", "tp", None, None),
        P("section", "tp", None, None),
        P("section", "tp", None, None),
        P("section", "tp"),
        P("section", "tp"),
        P("section", None),
        P("section", None),
    )
    out_specs = P("section", None, "tp")
    return jax.shard_map(local, mesh=mesh, in_specs=in_specs, out_specs=out_specs, check_vma=False)
```

```python
import functools

import jax
import jax.numpy as jnp
import numpy as np
from jax import lax
from jax.experimental import pallas as pl
from jax.experimental.pallas import tpu as pltpu
from jax.sharding import PartitionSpec as P

MESH = pl.DeviceIdType.MESH
F32, BF16, I32 = jnp.float32, jnp.bfloat16, jnp.int32

ROWS = 8
HEAD = 128
QUERY_HEADS = 32
KEY_HEADS = 8
HEADS = QUERY_HEADS + 2 * KEY_HEADS
PAGE = 64
BLOCKS = 4
PLANES = 16
NEAR = 16
SLOTS = 8
TOKENS = SLOTS * PAGE
SCALE = 1.0 / HEAD**0.5
MASKED = -1e30
LOWEST = -1e25
ROPE_BASE = 500000.0
LINE_ORDER = (8, 7, 9, 6, 10, 5, 11, 4, 12, 3, 13, 2, 14, 1, 15)
FARTHEST_FIRST = (7, 5, 3, 6, 1, 4, 2, 0)
SHIFTED_FARTHEST_FIRST = (7, 6, 5, 4, 3, 2, 1, 0)
TOGETHER = 2
X_LINE, X_PLANE, Q_LINE, Q_PLANE, PART_NEAR, PART_FAR, OUT_NEAR = range(7)


def nt(left, right):
    return lax.dot_general(
        left, right, (((1,), (1,)), ((), ())), preferred_element_type=F32
    )


def thirds(value):
    first = value.astype(BF16).astype(F32)
    rest = value - first
    second = rest.astype(BF16).astype(F32)
    return first, second, rest - second


def pack_stats(top, total, low, lane):
    slot = lane % (HEAD // 2) // 8
    pieces = thirds(top) + thirds(total)
    tiles = []
    for at in range(0, top.shape[0], 2 * ROWS):
        tile = jnp.zeros(lane.shape, F32)
        for k, piece in enumerate(pieces):
            pair = jnp.where(low, piece[at : at + ROWS], piece[at + ROWS : at + 2 * ROWS])
            tile = jnp.where(slot == k, pair, tile)
        tiles.append(tile.astype(BF16))
    return tiles


def merge(messages):
    stats = []
    for message in messages:
        tile = message[2].astype(F32)
        stats.append(tile + pltpu.roll(tile, HEAD - 8, 1) + pltpu.roll(tile, HEAD - 16, 1))
    top = functools.reduce(jnp.maximum, stats)
    total, sums = 0.0, [0.0, 0.0]
    for message, stat in zip(messages, stats):
        factor = jnp.exp(stat - top)
        total = total + factor * pltpu.roll(stat, HEAD - 24, 1)
        for h in range(2):
            scale = jnp.broadcast_to(factor[:, 64 * h : 64 * h + 1], stat.shape)
            sums[h] = sums[h] + scale * message[h].astype(F32)

    def stacked(stat):
        return jnp.concatenate([stat[:, 0:1], stat[:, 64:65]], axis=0)

    return stacked(top), stacked(total), jnp.concatenate(sums, axis=0)


def kernel(
    x_hbm,
    gain_hbm,
    wq_hbm,
    wo_hbm,
    key_hbm,
    value_hbm,
    scale_hbm,
    owner_hbm,
    number_hbm,
    length_hbm,
    row_hbm,
    freq_hbm,
    out_ref,
    x_own,
    gain,
    wq,
    wo,
    keys,
    values,
    scales,
    owner,
    number,
    length,
    row,
    freq,
    bias,
    turn,
    x_send,
    x_line,
    x_pack,
    x_all,
    q_send,
    q_line,
    q_pack,
    q_all,
    heads,
    part_send,
    part_all,
    sum_send,
    sum_all,
    att_send,
    att_all,
    local_sem,
    send_sem,
    recv_sem,
    group_sem,
):
    section = lax.axis_index("section")
    tp = lax.axis_index("tp")
    block, mine = tp // NEAR, tp % NEAR
    plane, place = tp // 4, tp % 4
    sections = lax.axis_size("section")
    after = lax.rem(section + 1, sections)
    before = lax.rem(section + sections - 1, sections)

    def near_id(other):
        return {"tp": block * NEAR + other}

    def far_id(other):
        return {"tp": other * NEAR + mine}

    def shifted_near_id(other):
        return {"section": after, "tp": block * NEAR + other}

    def line_id(other):
        return {"tp": other * 4 + place}

    def plane_id(where, other):
        return {"section": where, "tp": plane * 4 + other}

    barrier = pltpu.get_barrier_semaphore()

    def greet(device):
        pl.semaphore_signal(barrier, inc=1, device_id=device, device_id_type=MESH)

    for k in LINE_ORDER:
        greet(line_id(lax.rem(plane + k, PLANES)))
    for k in range(4):
        greet(plane_id(before, k))
    greetings = PLANES - 1 + 4

    moves = [
        pltpu.make_async_copy(src, dst, local_sem.at[k])
        for k, (src, dst) in enumerate(
            [
                (x_hbm, x_own),
                (row_hbm, row),
                (length_hbm, length),
                (owner_hbm, owner),
                (number_hbm, number),
                (scale_hbm, scales),
                (freq_hbm, freq),
                (key_hbm, keys),
                (value_hbm, values),
                (gain_hbm, gain),
                (wq_hbm, wq.at[pl.ds(0, 96)]),
                (wo_hbm, wo),
            ]
        )
    ]
    for move in moves:
        move.start()
    wq[96:128, :] = jnp.zeros((32, wq.shape[1]), BF16)

    moves[0].wait()
    x_here = x_own[...].astype(F32)
    x_send[...] = jnp.concatenate([x_here, x_here], axis=1).astype(BF16)

    lane = lax.broadcasted_iota(I32, (ROWS, HEAD), 1)
    low = lane < HEAD // 2

    def prepare():
        for k in range(1, 7):
            moves[k].wait()
        sub = lax.broadcasted_iota(I32, (ROWS, HEAD), 0)
        row_of = jnp.zeros((ROWS, HEAD), I32)
        limit = jnp.zeros((ROWS, HEAD), I32)
        for r in range(ROWS):
            request = row[0, r]
            row_of = jnp.where(sub == r, request, row_of)
            limit = jnp.where(sub == r, length[0, request], limit)
        for j in range(SLOTS // 2):
            tok_owner = jnp.where(low, owner[0, 2 * j], owner[0, 2 * j + 1])
            tok_page = jnp.where(low, number[0, 2 * j], number[0, 2 * j + 1])
            tok_pos = tok_page * PAGE + lane % PAGE
            seen = (tok_owner == row_of) & (tok_pos < limit)
            bias[:, HEAD * j : HEAD * (j + 1)] = jnp.where(seen, 0.0, MASKED)
        angle = limit.astype(F32) * freq[...]
        turn[0] = jnp.cos(angle)
        sine = jnp.sin(angle)
        turn[1] = jnp.where(low, -sine, sine)

        moves[7].wait()
        moves[8].wait()

        def restore(k, carry):
            at = pl.ds(pl.multiple_of(k * PAGE, PAGE), PAGE)
            both = scales[k]
            for which, store in ((0, keys), (1, values)):
                for g in range(KEY_HEADS):
                    cols = pl.ds(g * HEAD, HEAD)
                    factor = jnp.broadcast_to(both[which : which + 1, g : g + 1], (PAGE, HEAD))
                    store[at, cols] = (store[at, cols].astype(F32) * factor).astype(BF16)
            return carry

        lax.fori_loop(0, SLOTS, restore, 0)
        moves[9].wait()
        moves[10].wait()
        moves[11].wait()

    def send(stage, src, dst, device, sem=None):
        pltpu.make_async_remote_copy(
            src_ref=src,
            dst_ref=dst,
            send_sem=send_sem.at[stage],
            recv_sem=recv_sem.at[stage] if sem is None else sem,
            device_id=device,
            device_id_type=MESH,
        ).start()

    def start_far(stage, src, dst):
        for shift in (2, 1, 3):
            send(stage, src, dst.at[block], far_id(lax.rem(block + shift, BLOCKS)))

    chip, core = mine // 2, mine % 2
    sibling = 2 * chip + 1 - core

    def start_near(stage, src, dst):
        for k in FARTHEST_FIRST[:-1]:
            for other in (0, 1):
                send(stage, src, dst.at[mine], near_id(2 * (chip ^ k) + other))
        send(stage, src, dst.at[mine], near_id(sibling))

    def line_sem(stage, group):
        return group_sem.at[0 if stage == X_LINE else 1, group]

    def start_line(stage, src, dst):
        for k in LINE_ORDER:
            other = line_id(lax.rem(plane + k, PLANES))
            send(stage, src, dst.at[plane], other, line_sem(stage, block))

    def groups_of_line(stage, buffer):
        for shift in (0, 1, 3, 2):
            group = lax.rem(block + shift, BLOCKS)
            part = buffer.at[pl.ds(0, 4 if shift else 3)]
            pltpu.make_async_remote_copy(
                src_ref=part,
                dst_ref=part,
                send_sem=send_sem.at[stage],
                recv_sem=line_sem(stage, group),
                device_id=near_id(sibling),
                device_id_type=MESH,
            ).wait_recv()
            yield group, [buffer[4 * group + k].astype(F32) for k in range(4)]

    def start_plane(stage, where, src, dst):
        for k in (3, 2, 1, 0):
            send(stage, src, dst, plane_id(where, place ^ k))

    def all_of(stage, part):
        return pltpu.make_async_remote_copy(
            src_ref=part,
            dst_ref=part,
            send_sem=send_sem.at[stage],
            recv_sem=recv_sem.at[stage],
            device_id=near_id(sibling),
            device_id_type=MESH,
        )

    expected = {
        X_LINE: x_line.at[pl.ds(0, PLANES - 1)],
        X_PLANE: x_all,
        Q_LINE: q_line.at[pl.ds(0, PLANES - 1)],
        Q_PLANE: q_all,
        PART_NEAR: part_all,
        PART_FAR: sum_all.at[pl.ds(0, BLOCKS - 1)],
        OUT_NEAR: att_all.at[pl.ds(0, NEAR - 1)],
    }

    def arrived(stage):
        all_of(stage, expected[stage]).wait_recv()

    early = plane < PLANES // 2
    pl.when(early)(prepare)
    pl.semaphore_wait(barrier, greetings)

    start_line(X_LINE, x_send, x_line)
    x_line[plane] = x_send[...]
    pl.when(jnp.logical_not(early))(prepare)
    for group, blocks in groups_of_line(X_LINE, x_line):
        for u in range(2):
            x_pack[group, u] = jnp.where(low, blocks[2 * u], blocks[2 * u + 1]).astype(BF16)
        start_plane(X_PLANE, after, x_pack.at[group], x_all.at[place, group])
    arrived(X_PLANE)

    tiles = [None] * 32
    square = jnp.zeros((ROWS, HEAD), F32)
    for u in range(PLANES // 2):
        for j in range(2):
            even = x_all[2 * j, u // 2, u % 2].astype(F32)
            odd = x_all[2 * j + 1, u // 2, u % 2].astype(F32)
            square = square + even * even + odd * odd
            tiles[4 * u + j] = jnp.where(low, even, pltpu.roll(odd, 64, 1))
            tiles[4 * u + 2 + j] = jnp.where(low, pltpu.roll(even, 64, 1), odd)
    mean = jnp.sum(square, axis=1, keepdims=True) * (1.0 / 4096)
    shrink = lax.rsqrt(mean + 1e-05)
    normed = jnp.concatenate(
        [
            (tiles[t] * shrink * gain[:, HEAD * t : HEAD * (t + 1)]).astype(BF16)
            for t in range(32)
        ],
        axis=1,
    )
    columns = nt(normed, wq[...])
    turned = columns
    for k in range(1, 4):
        turned = jnp.where(place == k, pltpu.roll(columns, 96 * k % 128, 1), turned)
    q_send[...] = turned.astype(BF16)

    start_line(Q_LINE, q_send, q_line)
    q_line[plane] = q_send[...]
    quarter = lane // 32
    for group, blocks in groups_of_line(Q_LINE, q_line):
        for k in range(3):
            moved = pltpu.roll(blocks[3], 96 - 32 * k, 1)
            q_pack[group, k] = jnp.where(quarter == 3 - place, moved, blocks[k]).astype(BF16)
        start_plane(Q_PLANE, before, q_pack.at[group], q_all.at[place, group])
    arrived(Q_PLANE)

    cosine, sine = turn[0], turn[1]
    for c in range(BLOCKS):
        blocks = []
        for p in range(4):
            held = [q_all[p, c, k].astype(F32) for k in range(3)]
            fourth = pltpu.roll(held[0], 32, 1)
            for k in (1, 2):
                moved = pltpu.roll(held[k], 32 * (k + 1), 1)
                fourth = jnp.where(quarter == (4 - p + k) % 4, moved, fourth)
            blocks.append(held + [fourth])
        for z in range(4):
            for k, edge in enumerate((96, 64, 32)):
                h = 3 * (4 * c + z) + k
                head = jnp.where(lane < edge, blocks[k][z], blocks[k + 1][z])
                if h < QUERY_HEADS + KEY_HEADS:
                    head = head * cosine + pltpu.roll(head, 64, 1) * sine
                    head = head.astype(BF16).astype(F32)
                heads[h] = head

    hidden = jnp.concatenate([bias[...]] * 4, axis=0)
    for at in range(0, KEY_HEADS, TOGETHER):
        steps = SHIFTED_FARTHEST_FIRST[at : at + TOGETHER]
        groups = [chip ^ k for k in steps]
        cols = [pl.ds(pl.multiple_of(g * HEAD, HEAD), HEAD) for g in groups]
        queries = [heads[pl.ds(4 * g, 4)].reshape(4 * ROWS, HEAD).astype(BF16) for g in groups]
        scores = [nt(q, keys[:, c]) * SCALE + hidden for q, c in zip(queries, cols)]
        tops = [jnp.maximum(jnp.max(s, axis=1, keepdims=True), LOWEST) for s in scores]
        weights = [jnp.exp(s - t) for s, t in zip(scores, tops)]
        sums = [
            jnp.dot(w.astype(BF16), values[:, c], preferred_element_type=F32)
            for w, c in zip(weights, cols)
        ]
        totals = [jnp.sum(w, axis=1, keepdims=True) for w in weights]
        if steps[-1] == 0:
            new_key = jnp.concatenate([heads[QUERY_HEADS + chip]] * 4, axis=0)
            new_value = jnp.concatenate([heads[QUERY_HEADS + KEY_HEADS + chip]] * 4, axis=0)
            own = jnp.sum(queries[-1].astype(F32) * new_key, axis=1, keepdims=True) * SCALE
            pair = lax.broadcasted_iota(I32, (4 * ROWS, 1), 0) // (2 * ROWS)
            own = jnp.where((pair == core) & (block == 0), own, MASKED)
            top = jnp.maximum(tops[-1], own)
            old_weight, own_weight = jnp.exp(tops[-1] - top), jnp.exp(own - top)
            totals[-1] = totals[-1] * old_weight + own_weight
            sums[-1] = sums[-1] * old_weight + own_weight * new_value
            tops[-1] = top
        sums = [s.astype(BF16) for s in sums]
        for n, g in enumerate(groups):
            first, second = pack_stats(tops[n], totals[n], low, lane)
            for c, stats in ((0, first), (1, second)):
                part_send[2 * g + c, 0] = sums[n][16 * c : 16 * c + 8]
                part_send[2 * g + c, 1] = sums[n][16 * c + 8 : 16 * c + 16]
                part_send[2 * g + c, 2] = stats
        for g in groups:
            for other in (2 * g, 2 * g + 1):
                send(PART_NEAR, part_send.at[other], part_all.at[mine], shifted_near_id(other))

    arrived(PART_NEAR)
    top, total, weighted = merge([part_all[i] for i in range(NEAR)])
    sum_send[0] = weighted[:ROWS].astype(BF16)
    sum_send[1] = weighted[ROWS:].astype(BF16)
    sum_send[2] = pack_stats(top, total, low, lane)[0]

    start_far(PART_FAR, sum_send, sum_all)
    sum_all[block] = sum_send[...]
    arrived(PART_FAR)
    top, total, weighted = merge([sum_all[c] for c in range(BLOCKS)])
    att_send[...] = (weighted / total).astype(BF16)
    att_all[mine] = att_send[...]
    start_near(OUT_NEAR, att_send, att_all)
    arrived(OUT_NEAR)
    pieces = []
    for i in range(NEAR):
        pair = att_all[i].astype(F32)
        pieces += [pair[:ROWS], pair[ROWS:]]
    attended = jnp.concatenate(pieces, axis=1).astype(BF16)
    x_here = x_all[place, block, plane % 4 // 2].astype(F32)
    x_here = jnp.where(plane % 2 == 0, x_here, pltpu.roll(x_here, 64, 1))[:, :64]
    out_ref[...] = nt(attended, wo[...]) + x_here

    for stage, part in expected.items():
        all_of(stage, part).wait_send()


def local(x, gain, wq, wo, key_codes, value_codes, scale_table, owner, number, lengths, rows):
    half = HEAD // 2
    freq = ROPE_BASE ** (-np.arange(half, dtype=np.float64) / half)
    freq = jnp.asarray(np.concatenate([freq, freq]).astype(np.float32)[None, :])
    operands = (
        x[0],
        gain,
        jnp.swapaxes(wq[0], 0, 1),
        jnp.swapaxes(wo[0], 0, 1),
        key_codes[0].reshape(TOKENS, KEY_HEADS * HEAD),
        value_codes[0].reshape(TOKENS, KEY_HEADS * HEAD),
        scale_table[0],
        owner,
        number,
        lengths,
        rows,
        freq,
    )
    operands = [pltpu.with_memory_space_constraint(x, pltpu.HBM) for x in operands]
    vmem, smem = pltpu.VMEM, pltpu.SMEM
    out = pl.pallas_call(
        kernel,
        out_shape=vmem((ROWS, 64), F32),
        in_specs=[pl.BlockSpec(memory_space=pltpu.HBM)] * len(operands),
        out_specs=pl.BlockSpec(memory_space=pltpu.VMEM),
        scratch_shapes=[
            vmem((ROWS, 64), BF16),
            vmem((1, 4096), F32),
            vmem((128, 4096), BF16),
            vmem((64, 4096), BF16),
            vmem((TOKENS, 1024), BF16),
            vmem((TOKENS, 1024), BF16),
            vmem((SLOTS, 2, KEY_HEADS), F32),
            smem((1, SLOTS), I32),
            smem((1, SLOTS), I32),
            smem((1, 16), I32),
            smem((1, ROWS), I32),
            vmem((1, HEAD), F32),
            vmem((ROWS, TOKENS), F32),
            vmem((2, ROWS, HEAD), F32),
            vmem((ROWS, HEAD), BF16),
            vmem((PLANES, ROWS, HEAD), BF16),
            vmem((BLOCKS, 2, ROWS, HEAD), BF16),
            vmem((4, BLOCKS, 2, ROWS, HEAD), BF16),
            vmem((ROWS, HEAD), BF16),
            vmem((PLANES, ROWS, HEAD), BF16),
            vmem((BLOCKS, 3, ROWS, HEAD), BF16),
            vmem((4, BLOCKS, 3, ROWS, HEAD), BF16),
            vmem((HEADS, ROWS, HEAD), F32),
            vmem((NEAR, 3, ROWS, HEAD), BF16),
            vmem((NEAR, 3, ROWS, HEAD), BF16),
            vmem((3, ROWS, HEAD), BF16),
            vmem((BLOCKS, 3, ROWS, HEAD), BF16),
            vmem((2 * ROWS, HEAD), BF16),
            vmem((NEAR, 2 * ROWS, HEAD), BF16),
            pltpu.SemaphoreType.DMA((12,)),
            pltpu.SemaphoreType.DMA((7,)),
            pltpu.SemaphoreType.DMA((7,)),
            pltpu.SemaphoreType.DMA((2, BLOCKS)),
        ],
        compiler_params=pltpu.CompilerParams(
            collective_id=0, has_side_effects=True, vmem_limit_bytes=40 * 2**20
        ),
    )(*operands)
    return out[None]


def solution(mesh):
    in_specs = (
        P("section", None, "tp"),
        P("section", None),
        P("section", None, "tp"),
        P("section", None, "tp"),
        P("section", "tp", None, None),
        P("section", "tp", None, None),
        P("section", "tp", None, None),
        P("section", "tp"),
        P("section", "tp"),
        P("section", None),
        P("section", None),
    )
    out_specs = P("section", None, "tp")
    return jax.shard_map(local, mesh=mesh, in_specs=in_specs, out_specs=out_specs, check_vma=False)
```

```python
import functools

import jax
import jax.numpy as jnp
import numpy as np
from jax import lax
from jax.experimental import pallas as pl
from jax.experimental.pallas import tpu as pltpu
from jax.sharding import PartitionSpec as P

MESH = pl.DeviceIdType.MESH
F32, BF16, I32 = jnp.float32, jnp.bfloat16, jnp.int32

ROWS = 8
HEAD = 128
QUERY_HEADS = 32
KEY_HEADS = 8
HEADS = QUERY_HEADS + 2 * KEY_HEADS
PAGE = 64
BLOCKS = 4
PLANES = 16
NEAR = 16
SLOTS = 8
TOKENS = SLOTS * PAGE
SCALE = 1.0 / HEAD**0.5
MASKED = -1e30
LOWEST = -1e25
ROPE_BASE = 500000.0
LINE_ORDER = (8, 7, 9, 6, 10, 5, 11, 4, 12, 3, 13, 2, 14, 1, 15)
FARTHEST_FIRST = (7, 5, 3, 6, 1, 4, 2, 0)
SHIFTED_FARTHEST_FIRST = (7, 6, 5, 4, 3, 2, 1, 0)
TOGETHER = 2
X_LINE, X_PLANE, Q_LINE, Q_PLANE, PART_NEAR, PART_FAR, OUT_NEAR, PART_LEAD = range(8)
LEAD_SECTION, LEAD = 0, 1


def nt(left, right):
    return lax.dot_general(
        left, right, (((1,), (1,)), ((), ())), preferred_element_type=F32
    )


def thirds(value):
    first = value.astype(BF16).astype(F32)
    rest = value - first
    second = rest.astype(BF16).astype(F32)
    return first, second, rest - second


def pack_stats(top, total, low, lane):
    slot = lane % (HEAD // 2) // 8
    pieces = thirds(top) + thirds(total)
    tiles = []
    for at in range(0, top.shape[0], 2 * ROWS):
        tile = jnp.zeros(lane.shape, F32)
        for k, piece in enumerate(pieces):
            pair = jnp.where(low, piece[at : at + ROWS], piece[at + ROWS : at + 2 * ROWS])
            tile = jnp.where(slot == k, pair, tile)
        tiles.append(tile.astype(BF16))
    return tiles


def merge(messages):
    stats = []
    for message in messages:
        tile = message[2].astype(F32)
        stats.append(tile + pltpu.roll(tile, HEAD - 8, 1) + pltpu.roll(tile, HEAD - 16, 1))
    top = functools.reduce(jnp.maximum, stats)
    total, sums = 0.0, [0.0, 0.0]
    for message, stat in zip(messages, stats):
        factor = jnp.exp(stat - top)
        total = total + factor * pltpu.roll(stat, HEAD - 24, 1)
        for h in range(2):
            scale = jnp.broadcast_to(factor[:, 64 * h : 64 * h + 1], stat.shape)
            sums[h] = sums[h] + scale * message[h].astype(F32)

    def stacked(stat):
        return jnp.concatenate([stat[:, 0:1], stat[:, 64:65]], axis=0)

    return stacked(top), stacked(total), jnp.concatenate(sums, axis=0)


def kernel(
    x_hbm,
    gain_hbm,
    wq_hbm,
    wo_hbm,
    key_hbm,
    value_hbm,
    scale_hbm,
    owner_hbm,
    number_hbm,
    length_hbm,
    row_hbm,
    freq_hbm,
    out_ref,
    x_own,
    gain,
    wq,
    wo,
    keys,
    values,
    scales,
    owner,
    number,
    length,
    row,
    freq,
    bias,
    turn,
    x_send,
    x_line,
    x_pack,
    x_all,
    q_send,
    q_line,
    q_pack,
    q_all,
    heads,
    part_send,
    part_all,
    sum_send,
    sum_all,
    att_send,
    att_all,
    lead_all,
    local_sem,
    send_sem,
    recv_sem,
    group_sem,
):
    section = lax.axis_index("section")
    tp = lax.axis_index("tp")
    block, mine = tp // NEAR, tp % NEAR
    plane, place = tp // 4, tp % 4
    sections = lax.axis_size("section")
    after = lax.rem(section + 1, sections)
    before = lax.rem(section + sections - 1, sections)

    def near_id(other):
        return {"tp": block * NEAR + other}

    def far_id(other):
        return {"tp": other * NEAR + mine}

    def shifted_near_id(other):
        return {"section": after, "tp": block * NEAR + other}

    def line_id(other):
        return {"tp": other * 4 + place}

    def plane_id(where, other):
        return {"section": where, "tp": plane * 4 + other}

    barrier = pltpu.get_barrier_semaphore()

    def greet(device):
        pl.semaphore_signal(barrier, inc=1, device_id=device, device_id_type=MESH)

    for k in LINE_ORDER:
        greet(line_id(lax.rem(plane + k, PLANES)))
    for k in range(4):
        greet(plane_id(before, k))
    greetings = PLANES - 1 + 4

    moves = [
        pltpu.make_async_copy(src, dst, local_sem.at[k])
        for k, (src, dst) in enumerate(
            [
                (x_hbm, x_own),
                (row_hbm, row),
                (length_hbm, length),
                (owner_hbm, owner),
                (number_hbm, number),
                (scale_hbm, scales),
                (freq_hbm, freq),
                (key_hbm, keys),
                (value_hbm, values),
                (gain_hbm, gain),
                (wq_hbm, wq.at[pl.ds(0, 96)]),
                (wo_hbm, wo),
            ]
        )
    ]
    for move in moves:
        move.start()
    wq[96:128, :] = jnp.zeros((32, wq.shape[1]), BF16)

    moves[0].wait()
    x_here = x_own[...].astype(F32)
    x_send[...] = jnp.concatenate([x_here, x_here], axis=1).astype(BF16)

    lane = lax.broadcasted_iota(I32, (ROWS, HEAD), 1)
    low = lane < HEAD // 2

    def prepare():
        for k in range(1, 7):
            moves[k].wait()
        sub = lax.broadcasted_iota(I32, (ROWS, HEAD), 0)
        row_of = jnp.zeros((ROWS, HEAD), I32)
        limit = jnp.zeros((ROWS, HEAD), I32)
        for r in range(ROWS):
            request = row[0, r]
            row_of = jnp.where(sub == r, request, row_of)
            limit = jnp.where(sub == r, length[0, request], limit)
        for j in range(SLOTS // 2):
            tok_owner = jnp.where(low, owner[0, 2 * j], owner[0, 2 * j + 1])
            tok_page = jnp.where(low, number[0, 2 * j], number[0, 2 * j + 1])
            tok_pos = tok_page * PAGE + lane % PAGE
            seen = (tok_owner == row_of) & (tok_pos < limit)
            bias[:, HEAD * j : HEAD * (j + 1)] = jnp.where(seen, 0.0, MASKED)
        angle = limit.astype(F32) * freq[...]
        turn[0] = jnp.cos(angle)
        sine = jnp.sin(angle)
        turn[1] = jnp.where(low, -sine, sine)

        moves[7].wait()
        moves[8].wait()

        def restore(k, carry):
            at = pl.ds(pl.multiple_of(k * PAGE, PAGE), PAGE)
            both = scales[k]
            for which, store in ((0, keys), (1, values)):
                for g in range(KEY_HEADS):
                    cols = pl.ds(g * HEAD, HEAD)
                    factor = jnp.broadcast_to(both[which : which + 1, g : g + 1], (PAGE, HEAD))
                    store[at, cols] = (store[at, cols].astype(F32) * factor).astype(BF16)
            return carry

        lax.fori_loop(0, SLOTS, restore, 0)
        moves[9].wait()
        moves[10].wait()
        moves[11].wait()

    def send(stage, src, dst, device, sem=None):
        pltpu.make_async_remote_copy(
            src_ref=src,
            dst_ref=dst,
            send_sem=send_sem.at[stage],
            recv_sem=recv_sem.at[stage] if sem is None else sem,
            device_id=device,
            device_id_type=MESH,
        ).start()

    def start_far(stage, src, dst):
        for shift in (2, 1, 3):
            send(stage, src, dst.at[block], far_id(lax.rem(block + shift, BLOCKS)))

    chip, core = mine // 2, mine % 2
    sibling = 2 * chip + 1 - core

    lead_group = (section == LEAD_SECTION) & (block == LEAD // NEAR)
    is_lead = lead_group & (mine == LEAD % NEAR)

    def start_near(stage, src, dst):
        for k in FARTHEST_FIRST:
            for c in (0, 1):
                other = 2 * (chip ^ k) + c
                skipped = lead_group & (other == LEAD % NEAR) if c == LEAD % 2 else None
                if k == 0:
                    skipped = core == c if skipped is None else skipped | (core == c)
                if skipped is None:
                    send(stage, src, dst.at[mine], near_id(other))
                else:

                    @pl.when(jnp.logical_not(skipped))
                    def _():
                        send(stage, src, dst.at[mine], near_id(other))

    def line_sem(stage, group):
        return group_sem.at[0 if stage == X_LINE else 1, group]

    def start_line(stage, src, dst):
        for k in LINE_ORDER:
            other = line_id(lax.rem(plane + k, PLANES))
            send(stage, src, dst.at[plane], other, line_sem(stage, block))

    def groups_of_line(stage, buffer):
        for shift in (0, 1, 3, 2):
            group = lax.rem(block + shift, BLOCKS)
            part = buffer.at[pl.ds(0, 4 if shift else 3)]
            pltpu.make_async_remote_copy(
                src_ref=part,
                dst_ref=part,
                send_sem=send_sem.at[stage],
                recv_sem=line_sem(stage, group),
                device_id=near_id(sibling),
                device_id_type=MESH,
            ).wait_recv()
            yield group, [buffer[4 * group + k].astype(F32) for k in range(4)]

    def start_plane(stage, where, src, dst):
        for k in (3, 2, 1, 0):
            send(stage, src, dst, plane_id(where, place ^ k))

    def all_of(stage, part):
        return pltpu.make_async_remote_copy(
            src_ref=part,
            dst_ref=part,
            send_sem=send_sem.at[stage],
            recv_sem=recv_sem.at[stage],
            device_id=near_id(sibling),
            device_id_type=MESH,
        )

    expected = {
        X_LINE: x_line.at[pl.ds(0, PLANES - 1)],
        X_PLANE: x_all,
        Q_LINE: q_line.at[pl.ds(0, PLANES - 1)],
        Q_PLANE: q_all,
        PART_NEAR: part_all,
        PART_FAR: sum_all.at[pl.ds(0, BLOCKS - 1)],
        OUT_NEAR: att_all.at[pl.ds(0, NEAR - 1)],
    }

    def arrived(stage):
        all_of(stage, expected[stage]).wait_recv()

    early = plane < PLANES // 2
    pl.when(early)(prepare)
    pl.semaphore_wait(barrier, greetings)

    start_line(X_LINE, x_send, x_line)
    x_line[plane] = x_send[...]
    pl.when(jnp.logical_not(early))(prepare)
    for group, blocks in groups_of_line(X_LINE, x_line):
        for u in range(2):
            x_pack[group, u] = jnp.where(low, blocks[2 * u], blocks[2 * u + 1]).astype(BF16)
        start_plane(X_PLANE, after, x_pack.at[group], x_all.at[place, group])
    arrived(X_PLANE)

    tiles = [None] * 32
    square = jnp.zeros((ROWS, HEAD), F32)
    for u in range(PLANES // 2):
        for j in range(2):
            even = x_all[2 * j, u // 2, u % 2].astype(F32)
            odd = x_all[2 * j + 1, u // 2, u % 2].astype(F32)
            square = square + even * even + odd * odd
            tiles[4 * u + j] = jnp.where(low, even, pltpu.roll(odd, 64, 1))
            tiles[4 * u + 2 + j] = jnp.where(low, pltpu.roll(even, 64, 1), odd)
    mean = jnp.sum(square, axis=1, keepdims=True) * (1.0 / 4096)
    shrink = lax.rsqrt(mean + 1e-05)
    normed = jnp.concatenate(
        [
            (tiles[t] * shrink * gain[:, HEAD * t : HEAD * (t + 1)]).astype(BF16)
            for t in range(32)
        ],
        axis=1,
    )
    columns = nt(normed, wq[...])
    turned = columns
    for k in range(1, 4):
        turned = jnp.where(place == k, pltpu.roll(columns, 96 * k % 128, 1), turned)
    q_send[...] = turned.astype(BF16)

    start_line(Q_LINE, q_send, q_line)
    q_line[plane] = q_send[...]
    quarter = lane // 32
    for group, blocks in groups_of_line(Q_LINE, q_line):
        for k in range(3):
            moved = pltpu.roll(blocks[3], 96 - 32 * k, 1)
            q_pack[group, k] = jnp.where(quarter == 3 - place, moved, blocks[k]).astype(BF16)
        start_plane(Q_PLANE, before, q_pack.at[group], q_all.at[place, group])
    arrived(Q_PLANE)

    cosine, sine = turn[0], turn[1]
    for c in range(BLOCKS):
        blocks = []
        for p in range(4):
            held = [q_all[p, c, k].astype(F32) for k in range(3)]
            fourth = pltpu.roll(held[0], 32, 1)
            for k in (1, 2):
                moved = pltpu.roll(held[k], 32 * (k + 1), 1)
                fourth = jnp.where(quarter == (4 - p + k) % 4, moved, fourth)
            blocks.append(held + [fourth])
        for z in range(4):
            for k, edge in enumerate((96, 64, 32)):
                h = 3 * (4 * c + z) + k
                head = jnp.where(lane < edge, blocks[k][z], blocks[k + 1][z])
                if h < QUERY_HEADS + KEY_HEADS:
                    head = head * cosine + pltpu.roll(head, 64, 1) * sine
                    head = head.astype(BF16).astype(F32)
                heads[h] = head

    hidden = jnp.concatenate([bias[...]] * 4, axis=0)
    for at in range(0, KEY_HEADS, TOGETHER):
        steps = SHIFTED_FARTHEST_FIRST[at : at + TOGETHER]
        groups = [chip ^ k for k in steps]
        cols = [pl.ds(pl.multiple_of(g * HEAD, HEAD), HEAD) for g in groups]
        queries = [heads[pl.ds(4 * g, 4)].reshape(4 * ROWS, HEAD).astype(BF16) for g in groups]
        scores = [nt(q, keys[:, c]) * SCALE + hidden for q, c in zip(queries, cols)]
        tops = [jnp.maximum(jnp.max(s, axis=1, keepdims=True), LOWEST) for s in scores]
        weights = [jnp.exp(s - t) for s, t in zip(scores, tops)]
        sums = [
            jnp.dot(w.astype(BF16), values[:, c], preferred_element_type=F32)
            for w, c in zip(weights, cols)
        ]
        totals = [jnp.sum(w, axis=1, keepdims=True) for w in weights]
        if steps[-1] == 0:
            new_key = jnp.concatenate([heads[QUERY_HEADS + chip]] * 4, axis=0)
            new_value = jnp.concatenate([heads[QUERY_HEADS + KEY_HEADS + chip]] * 4, axis=0)
            own = jnp.sum(queries[-1].astype(F32) * new_key, axis=1, keepdims=True) * SCALE
            pair = lax.broadcasted_iota(I32, (4 * ROWS, 1), 0) // (2 * ROWS)
            own = jnp.where((pair == core) & (block == 0), own, MASKED)
            top = jnp.maximum(tops[-1], own)
            old_weight, own_weight = jnp.exp(tops[-1] - top), jnp.exp(own - top)
            totals[-1] = totals[-1] * old_weight + own_weight
            sums[-1] = sums[-1] * old_weight + own_weight * new_value
            tops[-1] = top
        sums = [s.astype(BF16) for s in sums]
        for n, g in enumerate(groups):
            first, second = pack_stats(tops[n], totals[n], low, lane)
            for c, stats in ((0, first), (1, second)):
                part_send[2 * g + c, 0] = sums[n][16 * c : 16 * c + 8]
                part_send[2 * g + c, 1] = sums[n][16 * c + 8 : 16 * c + 16]
                part_send[2 * g + c, 2] = stats
        for g in groups:
            for other in (2 * g, 2 * g + 1):
                send(PART_NEAR, part_send.at[other], part_all.at[mine], shifted_near_id(other))

    arrived(PART_NEAR)
    top, total, weighted = merge([part_all[i] for i in range(NEAR)])
    sum_send[0] = weighted[:ROWS].astype(BF16)
    sum_send[1] = weighted[ROWS:].astype(BF16)
    sum_send[2] = pack_stats(top, total, low, lane)[0]

    start_far(PART_FAR, sum_send, sum_all)
    to_lead = (section == LEAD_SECTION) & (tp != LEAD)

    @pl.when(to_lead)
    def _():
        send(PART_LEAD, sum_send, lead_all.at[tp], {"tp": LEAD})

    sum_all[block] = sum_send[...]
    arrived(PART_FAR)
    top, total, weighted = merge([sum_all[c] for c in range(BLOCKS)])
    att_send[...] = (weighted / total).astype(BF16)
    att_all[mine] = att_send[...]
    start_near(OUT_NEAR, att_send, att_all)

    @pl.when(jnp.logical_not(is_lead))
    def _():
        arrived(OUT_NEAR)

    @pl.when(is_lead)
    def _():
        lead_all[LEAD] = sum_send[...]
        all_of(PART_LEAD, lead_all.at[pl.ds(0, BLOCKS * NEAR - 1)]).wait_recv()
        for i in range(NEAR):
            _, total, weighted = merge([lead_all[NEAR * c + i] for c in range(BLOCKS)])
            att_all[i] = (weighted / total).astype(BF16)

    pieces = []
    for i in range(NEAR):
        pair = att_all[i].astype(F32)
        pieces += [pair[:ROWS], pair[ROWS:]]
    attended = jnp.concatenate(pieces, axis=1).astype(BF16)
    x_here = x_all[place, block, plane % 4 // 2].astype(F32)
    x_here = jnp.where(plane % 2 == 0, x_here, pltpu.roll(x_here, 64, 1))[:, :64]
    out_ref[...] = nt(attended, wo[...]) + x_here

    for stage, part in expected.items():
        if stage != OUT_NEAR:
            all_of(stage, part).wait_send()
    fewer = lead_group & jnp.logical_not(is_lead)

    @pl.when(fewer)
    def _():
        all_of(OUT_NEAR, att_all.at[pl.ds(0, NEAR - 2)]).wait_send()

    @pl.when(jnp.logical_not(fewer))
    def _():
        all_of(OUT_NEAR, att_all.at[pl.ds(0, NEAR - 1)]).wait_send()

    @pl.when(to_lead)
    def _():
        all_of(PART_LEAD, sum_send).wait_send()


def local(x, gain, wq, wo, key_codes, value_codes, scale_table, owner, number, lengths, rows):
    half = HEAD // 2
    freq = ROPE_BASE ** (-np.arange(half, dtype=np.float64) / half)
    freq = jnp.asarray(np.concatenate([freq, freq]).astype(np.float32)[None, :])
    operands = (
        x[0],
        gain,
        jnp.swapaxes(wq[0], 0, 1),
        jnp.swapaxes(wo[0], 0, 1),
        key_codes[0].reshape(TOKENS, KEY_HEADS * HEAD),
        value_codes[0].reshape(TOKENS, KEY_HEADS * HEAD),
        scale_table[0],
        owner,
        number,
        lengths,
        rows,
        freq,
    )
    operands = [pltpu.with_memory_space_constraint(x, pltpu.HBM) for x in operands]
    vmem, smem = pltpu.VMEM, pltpu.SMEM
    out = pl.pallas_call(
        kernel,
        out_shape=vmem((ROWS, 64), F32),
        in_specs=[pl.BlockSpec(memory_space=pltpu.HBM)] * len(operands),
        out_specs=pl.BlockSpec(memory_space=pltpu.VMEM),
        scratch_shapes=[
            vmem((ROWS, 64), BF16),
            vmem((1, 4096), F32),
            vmem((128, 4096), BF16),
            vmem((64, 4096), BF16),
            vmem((TOKENS, 1024), BF16),
            vmem((TOKENS, 1024), BF16),
            vmem((SLOTS, 2, KEY_HEADS), F32),
            smem((1, SLOTS), I32),
            smem((1, SLOTS), I32),
            smem((1, 16), I32),
            smem((1, ROWS), I32),
            vmem((1, HEAD), F32),
            vmem((ROWS, TOKENS), F32),
            vmem((2, ROWS, HEAD), F32),
            vmem((ROWS, HEAD), BF16),
            vmem((PLANES, ROWS, HEAD), BF16),
            vmem((BLOCKS, 2, ROWS, HEAD), BF16),
            vmem((4, BLOCKS, 2, ROWS, HEAD), BF16),
            vmem((ROWS, HEAD), BF16),
            vmem((PLANES, ROWS, HEAD), BF16),
            vmem((BLOCKS, 3, ROWS, HEAD), BF16),
            vmem((4, BLOCKS, 3, ROWS, HEAD), BF16),
            vmem((HEADS, ROWS, HEAD), F32),
            vmem((NEAR, 3, ROWS, HEAD), BF16),
            vmem((NEAR, 3, ROWS, HEAD), BF16),
            vmem((3, ROWS, HEAD), BF16),
            vmem((BLOCKS, 3, ROWS, HEAD), BF16),
            vmem((2 * ROWS, HEAD), BF16),
            vmem((NEAR, 2 * ROWS, HEAD), BF16),
            vmem((BLOCKS * NEAR, 3, ROWS, HEAD), BF16),
            pltpu.SemaphoreType.DMA((12,)),
            pltpu.SemaphoreType.DMA((8,)),
            pltpu.SemaphoreType.DMA((8,)),
            pltpu.SemaphoreType.DMA((2, BLOCKS)),
        ],
        compiler_params=pltpu.CompilerParams(
            collective_id=0, has_side_effects=True, vmem_limit_bytes=40 * 2**20
        ),
    )(*operands)
    return out[None]


def solution(mesh):
    in_specs = (
        P("section", None, "tp"),
        P("section", None),
        P("section", None, "tp"),
        P("section", None, "tp"),
        P("section", "tp", None, None),
        P("section", "tp", None, None),
        P("section", "tp", None, None),
        P("section", "tp"),
        P("section", "tp"),
        P("section", None),
        P("section", None),
    )
    out_specs = P("section", None, "tp")
    return jax.shard_map(local, mesh=mesh, in_specs=in_specs, out_specs=out_specs, check_vma=False)
```

```python
import functools

import jax
import jax.numpy as jnp
import numpy as np
from jax import lax
from jax.experimental import pallas as pl
from jax.experimental.pallas import tpu as pltpu
from jax.sharding import PartitionSpec as P

MESH = pl.DeviceIdType.MESH
F32, BF16, I32 = jnp.float32, jnp.bfloat16, jnp.int32

ROWS = 8
HEAD = 128
QUERY_HEADS = 32
KEY_HEADS = 8
HEADS = QUERY_HEADS + 2 * KEY_HEADS
PAGE = 64
BLOCKS = 4
PLANES = 16
NEAR = 16
SLOTS = 8
TOKENS = SLOTS * PAGE
SCALE = 1.0 / HEAD**0.5
MASKED = -1e30
LOWEST = -1e25
ROPE_BASE = 500000.0
LINE_ORDER = (8, 7, 9, 6, 10, 5, 11, 4, 12, 3, 13, 2, 14, 1, 15)
FARTHEST_FIRST = (7, 5, 3, 6, 1, 4, 2, 0)
X_LINE, X_PLANE, Q_LINE, Q_PLANE, PART_NEAR, PART_FAR, OUT_NEAR, PART_LEAD = range(8)
LEAD_SECTION, LEAD = 0, 1


def nt(left, right):
    return lax.dot_general(
        left, right, (((1,), (1,)), ((), ())), preferred_element_type=F32
    )


def thirds(value):
    first = value.astype(BF16).astype(F32)
    rest = value - first
    second = rest.astype(BF16).astype(F32)
    return first, second, rest - second


def pack_stats(top, total, low, lane):
    slot = lane % (HEAD // 2) // 8
    pieces = thirds(top) + thirds(total)
    tiles = []
    for at in range(0, top.shape[0], 2 * ROWS):
        tile = jnp.zeros(lane.shape, F32)
        for k, piece in enumerate(pieces):
            pair = jnp.where(low, piece[at : at + ROWS], piece[at + ROWS : at + 2 * ROWS])
            tile = jnp.where(slot == k, pair, tile)
        tiles.append(tile.astype(BF16))
    return tiles


def merge(messages):
    stats = []
    for message in messages:
        tile = message[2].astype(F32)
        stats.append(tile + pltpu.roll(tile, HEAD - 8, 1) + pltpu.roll(tile, HEAD - 16, 1))
    top = functools.reduce(jnp.maximum, stats)
    total, sums = 0.0, [0.0, 0.0]
    for message, stat in zip(messages, stats):
        factor = jnp.exp(stat - top)
        total = total + factor * pltpu.roll(stat, HEAD - 24, 1)
        for h in range(2):
            scale = jnp.broadcast_to(factor[:, 64 * h : 64 * h + 1], stat.shape)
            sums[h] = sums[h] + scale * message[h].astype(F32)

    def stacked(stat):
        return jnp.concatenate([stat[:, 0:1], stat[:, 64:65]], axis=0)

    return stacked(top), stacked(total), jnp.concatenate(sums, axis=0)


def kernel(
    x_hbm,
    gain_hbm,
    wq_hbm,
    wo_hbm,
    key_hbm,
    value_hbm,
    scale_hbm,
    owner_hbm,
    number_hbm,
    length_hbm,
    row_hbm,
    freq_hbm,
    out_ref,
    x_own,
    gain,
    wq,
    wo,
    keys,
    values,
    scales,
    owner,
    number,
    length,
    row,
    freq,
    bias,
    turn,
    x_send,
    x_line,
    x_pack,
    x_all,
    q_send,
    q_line,
    q_pack,
    q_all,
    heads,
    part_send,
    part_all,
    sum_send,
    sum_all,
    att_send,
    att_all,
    lead_all,
    local_sem,
    send_sem,
    recv_sem,
    group_sem,
):
    section = lax.axis_index("section")
    tp = lax.axis_index("tp")
    block, mine = tp // NEAR, tp % NEAR
    plane, place = tp // 4, tp % 4
    sections = lax.axis_size("section")
    after = lax.rem(section + 1, sections)
    before = lax.rem(section + sections - 1, sections)

    def near_id(other):
        return {"tp": block * NEAR + other}

    def far_id(other):
        return {"tp": other * NEAR + mine}

    def shifted_near_id(other):
        return {"section": after, "tp": block * NEAR + other}

    def line_id(other):
        return {"tp": other * 4 + place}

    def plane_id(where, other):
        return {"section": where, "tp": plane * 4 + other}

    barrier = pltpu.get_barrier_semaphore()

    def greet(device):
        pl.semaphore_signal(barrier, inc=1, device_id=device, device_id_type=MESH)

    for k in LINE_ORDER:
        greet(line_id(lax.rem(plane + k, PLANES)))
    for k in range(4):
        greet(plane_id(before, k))
    greetings = PLANES - 1 + 4

    moves = [
        pltpu.make_async_copy(src, dst, local_sem.at[k])
        for k, (src, dst) in enumerate(
            [
                (x_hbm, x_own),
                (row_hbm, row),
                (length_hbm, length),
                (owner_hbm, owner),
                (number_hbm, number),
                (scale_hbm, scales),
                (freq_hbm, freq),
                (key_hbm, keys),
                (value_hbm, values),
                (gain_hbm, gain),
                (wq_hbm, wq.at[pl.ds(0, 96)]),
                (wo_hbm, wo),
            ]
        )
    ]
    for move in moves:
        move.start()
    wq[96:128, :] = jnp.zeros((32, wq.shape[1]), BF16)

    moves[0].wait()
    x_here = x_own[...].astype(F32)
    x_send[...] = jnp.concatenate([x_here, x_here], axis=1).astype(BF16)

    lane = lax.broadcasted_iota(I32, (ROWS, HEAD), 1)
    low = lane < HEAD // 2

    def prepare():
        for k in range(1, 7):
            moves[k].wait()
        sub = lax.broadcasted_iota(I32, (ROWS, HEAD), 0)
        row_of = jnp.zeros((ROWS, HEAD), I32)
        limit = jnp.zeros((ROWS, HEAD), I32)
        for r in range(ROWS):
            request = row[0, r]
            row_of = jnp.where(sub == r, request, row_of)
            limit = jnp.where(sub == r, length[0, request], limit)
        for j in range(SLOTS // 2):
            tok_owner = jnp.where(low, owner[0, 2 * j], owner[0, 2 * j + 1])
            tok_page = jnp.where(low, number[0, 2 * j], number[0, 2 * j + 1])
            tok_pos = tok_page * PAGE + lane % PAGE
            seen = (tok_owner == row_of) & (tok_pos < limit)
            bias[:, HEAD * j : HEAD * (j + 1)] = jnp.where(seen, 0.0, MASKED)
        angle = limit.astype(F32) * freq[...]
        turn[0] = jnp.cos(angle)
        sine = jnp.sin(angle)
        turn[1] = jnp.where(low, -sine, sine)

        moves[7].wait()
        moves[8].wait()

        def restore(k, carry):
            at = pl.ds(pl.multiple_of(k * PAGE, PAGE), PAGE)
            both = scales[k]
            for which, store in ((0, keys), (1, values)):
                for g in range(KEY_HEADS):
                    cols = pl.ds(g * HEAD, HEAD)
                    factor = jnp.broadcast_to(both[which : which + 1, g : g + 1], (PAGE, HEAD))
                    store[at, cols] = (store[at, cols].astype(F32) * factor).astype(BF16)
            return carry

        lax.fori_loop(0, SLOTS, restore, 0)
        moves[9].wait()
        moves[10].wait()
        moves[11].wait()

    def send(stage, src, dst, device, sem=None):
        pltpu.make_async_remote_copy(
            src_ref=src,
            dst_ref=dst,
            send_sem=send_sem.at[stage],
            recv_sem=recv_sem.at[stage] if sem is None else sem,
            device_id=device,
            device_id_type=MESH,
        ).start()

    def start_far(stage, src, dst):
        for shift in (2, 1, 3):
            send(stage, src, dst.at[block], far_id(lax.rem(block + shift, BLOCKS)))

    chip, core = mine // 2, mine % 2
    sibling = 2 * chip + 1 - core

    lead_group = (section == LEAD_SECTION) & (block == LEAD // NEAR)
    is_lead = lead_group & (mine == LEAD % NEAR)

    def start_near(stage, src, dst):
        for k in FARTHEST_FIRST:
            for c in (0, 1):
                other = 2 * (chip ^ k) + c
                skipped = lead_group & (other == LEAD % NEAR) if c == LEAD % 2 else None
                if k == 0:
                    skipped = core == c if skipped is None else skipped | (core == c)
                if skipped is None:
                    send(stage, src, dst.at[mine], near_id(other))
                else:

                    @pl.when(jnp.logical_not(skipped))
                    def _():
                        send(stage, src, dst.at[mine], near_id(other))

    def line_sem(stage, group):
        return group_sem.at[0 if stage == X_LINE else 1, group]

    def start_line(stage, src, dst):
        for k in LINE_ORDER:
            other = line_id(lax.rem(plane + k, PLANES))
            send(stage, src, dst.at[plane], other, line_sem(stage, block))

    def groups_of_line(stage, buffer):
        for shift in (0, 1, 3, 2):
            group = lax.rem(block + shift, BLOCKS)
            part = buffer.at[pl.ds(0, 4 if shift else 3)]
            pltpu.make_async_remote_copy(
                src_ref=part,
                dst_ref=part,
                send_sem=send_sem.at[stage],
                recv_sem=line_sem(stage, group),
                device_id=near_id(sibling),
                device_id_type=MESH,
            ).wait_recv()
            yield group, [buffer[4 * group + k].astype(F32) for k in range(4)]

    def start_plane(stage, where, src, dst):
        for k in (3, 2, 1, 0):
            send(stage, src, dst, plane_id(where, place ^ k))

    def all_of(stage, part):
        return pltpu.make_async_remote_copy(
            src_ref=part,
            dst_ref=part,
            send_sem=send_sem.at[stage],
            recv_sem=recv_sem.at[stage],
            device_id=near_id(sibling),
            device_id_type=MESH,
        )

    expected = {
        X_LINE: x_line.at[pl.ds(0, PLANES - 1)],
        X_PLANE: x_all,
        Q_LINE: q_line.at[pl.ds(0, PLANES - 1)],
        Q_PLANE: q_all,
        PART_NEAR: part_all,
        PART_FAR: sum_all.at[pl.ds(0, BLOCKS - 1)],
        OUT_NEAR: att_all.at[pl.ds(0, NEAR - 1)],
    }

    def arrived(stage):
        all_of(stage, expected[stage]).wait_recv()

    early = plane < PLANES // 2
    pl.when(early)(prepare)
    pl.semaphore_wait(barrier, greetings)

    start_line(X_LINE, x_send, x_line)
    x_line[plane] = x_send[...]
    pl.when(jnp.logical_not(early))(prepare)
    for group, blocks in groups_of_line(X_LINE, x_line):
        for u in range(2):
            x_pack[group, u] = jnp.where(low, blocks[2 * u], blocks[2 * u + 1]).astype(BF16)
        start_plane(X_PLANE, after, x_pack.at[group], x_all.at[place, group])
    arrived(X_PLANE)

    tiles = [None] * 32
    square = jnp.zeros((ROWS, HEAD), F32)
    for u in range(PLANES // 2):
        for j in range(2):
            even = x_all[2 * j, u // 2, u % 2].astype(F32)
            odd = x_all[2 * j + 1, u // 2, u % 2].astype(F32)
            square = square + even * even + odd * odd
            tiles[4 * u + j] = jnp.where(low, even, pltpu.roll(odd, 64, 1))
            tiles[4 * u + 2 + j] = jnp.where(low, pltpu.roll(even, 64, 1), odd)
    mean = jnp.sum(square, axis=1, keepdims=True) * (1.0 / 4096)
    shrink = lax.rsqrt(mean + 1e-05)
    normed = jnp.concatenate(
        [
            (tiles[t] * shrink * gain[:, HEAD * t : HEAD * (t + 1)]).astype(BF16)
            for t in range(32)
        ],
        axis=1,
    )
    columns = nt(normed, wq[...])
    turned = columns
    for k in range(1, 4):
        turned = jnp.where(place == k, pltpu.roll(columns, 96 * k % 128, 1), turned)
    q_send[...] = turned.astype(BF16)

    start_line(Q_LINE, q_send, q_line)
    q_line[plane] = q_send[...]
    quarter = lane // 32
    for group, blocks in groups_of_line(Q_LINE, q_line):
        for k in range(3):
            moved = pltpu.roll(blocks[3], 96 - 32 * k, 1)
            q_pack[group, k] = jnp.where(quarter == 3 - place, moved, blocks[k]).astype(BF16)
        start_plane(Q_PLANE, before, q_pack.at[group], q_all.at[place, group])
    arrived(Q_PLANE)

    cosine, sine = turn[0], turn[1]
    for c in range(BLOCKS):
        blocks = []
        for p in range(4):
            held = [q_all[p, c, k].astype(F32) for k in range(3)]
            fourth = pltpu.roll(held[0], 32, 1)
            for k in (1, 2):
                moved = pltpu.roll(held[k], 32 * (k + 1), 1)
                fourth = jnp.where(quarter == (4 - p + k) % 4, moved, fourth)
            blocks.append(held + [fourth])
        for z in range(4):
            for k, edge in enumerate((96, 64, 32)):
                h = 3 * (4 * c + z) + k
                head = jnp.where(lane < edge, blocks[k][z], blocks[k + 1][z])
                if h < QUERY_HEADS + KEY_HEADS:
                    head = head * cosine + pltpu.roll(head, 64, 1) * sine
                    head = head.astype(BF16).astype(F32)
                heads[h] = head

    hidden = jnp.concatenate([bias[...]] * 8, axis=0)
    blank = jnp.zeros((4 * ROWS, HEAD), F32)
    for step in (3, 2, 1, 0):
        pair = (chip // 2) ^ step
        cols = pl.ds(pl.multiple_of(pair * 2 * HEAD, 2 * HEAD), 2 * HEAD)
        rows = heads[pl.ds(8 * pair, 8)].reshape(8 * ROWS, HEAD)
        query = jnp.concatenate(
            [
                jnp.concatenate([rows[: 4 * ROWS], blank], axis=1),
                jnp.concatenate([blank, rows[4 * ROWS :]], axis=1),
            ],
            axis=0,
        ).astype(BF16)
        score = nt(query, keys[:, cols]) * SCALE + hidden
        top = jnp.maximum(jnp.max(score, axis=1, keepdims=True), LOWEST)
        weight = jnp.exp(score - top)
        both = jnp.dot(weight.astype(BF16), values[:, cols], preferred_element_type=F32)
        weighted = jnp.concatenate([both[: 4 * ROWS, :HEAD], both[4 * ROWS :, HEAD:]], axis=0)
        total = jnp.sum(weight, axis=1, keepdims=True)
        if step == 0:
            key = QUERY_HEADS + 2 * pair
            new_key = jnp.concatenate([heads[key]] * 4 + [heads[key + 1]] * 4, axis=0)
            key = key + KEY_HEADS
            new_value = jnp.concatenate([heads[key]] * 4 + [heads[key + 1]] * 4, axis=0)
            own = jnp.sum(rows * new_key, axis=1, keepdims=True) * SCALE
            place_of = lax.broadcasted_iota(I32, (8 * ROWS, 1), 0) // (2 * ROWS)
            own = jnp.where((place_of == mine % 4) & (block == 0), own, MASKED)
            peak = jnp.maximum(top, own)
            old_weight, own_weight = jnp.exp(top - peak), jnp.exp(own - peak)
            total = total * old_weight + own_weight
            weighted = weighted * old_weight + own_weight * new_value
            top = peak
        weighted = weighted.astype(BF16)
        for n, stats in enumerate(pack_stats(top, total, low, lane)):
            part_send[4 * pair + n, 0] = weighted[16 * n : 16 * n + 8]
            part_send[4 * pair + n, 1] = weighted[16 * n + 8 : 16 * n + 16]
            part_send[4 * pair + n, 2] = stats
        for n in range(4):
            other = 4 * pair + n
            send(PART_NEAR, part_send.at[other], part_all.at[mine], shifted_near_id(other))

    arrived(PART_NEAR)
    top, total, weighted = merge([part_all[i] for i in range(NEAR)])
    sum_send[0] = weighted[:ROWS].astype(BF16)
    sum_send[1] = weighted[ROWS:].astype(BF16)
    sum_send[2] = pack_stats(top, total, low, lane)[0]

    start_far(PART_FAR, sum_send, sum_all)
    to_lead = (section == LEAD_SECTION) & (tp != LEAD)

    @pl.when(to_lead)
    def _():
        send(PART_LEAD, sum_send, lead_all.at[tp], {"tp": LEAD})

    sum_all[block] = sum_send[...]
    arrived(PART_FAR)
    top, total, weighted = merge([sum_all[c] for c in range(BLOCKS)])
    att_send[...] = (weighted / total).astype(BF16)
    att_all[mine] = att_send[...]
    start_near(OUT_NEAR, att_send, att_all)

    @pl.when(jnp.logical_not(is_lead))
    def _():
        arrived(OUT_NEAR)

    @pl.when(is_lead)
    def _():
        lead_all[LEAD] = sum_send[...]
        all_of(PART_LEAD, lead_all.at[pl.ds(0, BLOCKS * NEAR - 1)]).wait_recv()
        for i in range(NEAR):
            _, total, weighted = merge([lead_all[NEAR * c + i] for c in range(BLOCKS)])
            att_all[i] = (weighted / total).astype(BF16)

    pieces = []
    for i in range(NEAR):
        pair = att_all[i].astype(F32)
        pieces += [pair[:ROWS], pair[ROWS:]]
    attended = jnp.concatenate(pieces, axis=1).astype(BF16)
    x_here = x_all[place, block, plane % 4 // 2].astype(F32)
    x_here = jnp.where(plane % 2 == 0, x_here, pltpu.roll(x_here, 64, 1))[:, :64]
    out_ref[...] = nt(attended, wo[...]) + x_here

    for stage, part in expected.items():
        if stage != OUT_NEAR:
            all_of(stage, part).wait_send()
    fewer = lead_group & jnp.logical_not(is_lead)

    @pl.when(fewer)
    def _():
        all_of(OUT_NEAR, att_all.at[pl.ds(0, NEAR - 2)]).wait_send()

    @pl.when(jnp.logical_not(fewer))
    def _():
        all_of(OUT_NEAR, att_all.at[pl.ds(0, NEAR - 1)]).wait_send()

    @pl.when(to_lead)
    def _():
        all_of(PART_LEAD, sum_send).wait_send()


def local(x, gain, wq, wo, key_codes, value_codes, scale_table, owner, number, lengths, rows):
    half = HEAD // 2
    freq = ROPE_BASE ** (-np.arange(half, dtype=np.float64) / half)
    freq = jnp.asarray(np.concatenate([freq, freq]).astype(np.float32)[None, :])
    operands = (
        x[0],
        gain,
        jnp.swapaxes(wq[0], 0, 1),
        jnp.swapaxes(wo[0], 0, 1),
        key_codes[0].reshape(TOKENS, KEY_HEADS * HEAD),
        value_codes[0].reshape(TOKENS, KEY_HEADS * HEAD),
        scale_table[0],
        owner,
        number,
        lengths,
        rows,
        freq,
    )
    operands = [pltpu.with_memory_space_constraint(x, pltpu.HBM) for x in operands]
    vmem, smem = pltpu.VMEM, pltpu.SMEM
    out = pl.pallas_call(
        kernel,
        out_shape=vmem((ROWS, 64), F32),
        in_specs=[pl.BlockSpec(memory_space=pltpu.HBM)] * len(operands),
        out_specs=pl.BlockSpec(memory_space=pltpu.VMEM),
        scratch_shapes=[
            vmem((ROWS, 64), BF16),
            vmem((1, 4096), F32),
            vmem((128, 4096), BF16),
            vmem((64, 4096), BF16),
            vmem((TOKENS, 1024), BF16),
            vmem((TOKENS, 1024), BF16),
            vmem((SLOTS, 2, KEY_HEADS), F32),
            smem((1, SLOTS), I32),
            smem((1, SLOTS), I32),
            smem((1, 16), I32),
            smem((1, ROWS), I32),
            vmem((1, HEAD), F32),
            vmem((ROWS, TOKENS), F32),
            vmem((2, ROWS, HEAD), F32),
            vmem((ROWS, HEAD), BF16),
            vmem((PLANES, ROWS, HEAD), BF16),
            vmem((BLOCKS, 2, ROWS, HEAD), BF16),
            vmem((4, BLOCKS, 2, ROWS, HEAD), BF16),
            vmem((ROWS, HEAD), BF16),
            vmem((PLANES, ROWS, HEAD), BF16),
            vmem((BLOCKS, 3, ROWS, HEAD), BF16),
            vmem((4, BLOCKS, 3, ROWS, HEAD), BF16),
            vmem((HEADS, ROWS, HEAD), F32),
            vmem((NEAR, 3, ROWS, HEAD), BF16),
            vmem((NEAR, 3, ROWS, HEAD), BF16),
            vmem((3, ROWS, HEAD), BF16),
            vmem((BLOCKS, 3, ROWS, HEAD), BF16),
            vmem((2 * ROWS, HEAD), BF16),
            vmem((NEAR, 2 * ROWS, HEAD), BF16),
            vmem((BLOCKS * NEAR, 3, ROWS, HEAD), BF16),
            pltpu.SemaphoreType.DMA((12,)),
            pltpu.SemaphoreType.DMA((8,)),
            pltpu.SemaphoreType.DMA((8,)),
            pltpu.SemaphoreType.DMA((2, BLOCKS)),
        ],
        compiler_params=pltpu.CompilerParams(
            collective_id=0, has_side_effects=True, vmem_limit_bytes=40 * 2**20
        ),
    )(*operands)
    return out[None]


def solution(mesh):
    in_specs = (
        P("section", None, "tp"),
        P("section", None),
        P("section", None, "tp"),
        P("section", None, "tp"),
        P("section", "tp", None, None),
        P("section", "tp", None, None),
        P("section", "tp", None, None),
        P("section", "tp"),
        P("section", "tp"),
        P("section", None),
        P("section", None),
    )
    out_specs = P("section", None, "tp")
    return jax.shard_map(local, mesh=mesh, in_specs=in_specs, out_specs=out_specs, check_vma=False)
```

```python
import functools

import jax
import jax.numpy as jnp
import numpy as np
from jax import lax
from jax.experimental import pallas as pl
from jax.experimental.pallas import tpu as pltpu
from jax.sharding import PartitionSpec as P

MESH = pl.DeviceIdType.MESH
F32, BF16, I32 = jnp.float32, jnp.bfloat16, jnp.int32

ROWS = 8
HEAD = 128
QUERY_HEADS = 32
KEY_HEADS = 8
HEADS = QUERY_HEADS + 2 * KEY_HEADS
PAGE = 64
BLOCKS = 4
PLANES = 16
NEAR = 16
SLOTS = 8
TOKENS = SLOTS * PAGE
SCALE = 1.0 / HEAD**0.5
MASKED = -1e30
LOWEST = -1e25
ROPE_BASE = 500000.0
LINE_ORDER = (8, 7, 9, 6, 10, 5, 11, 4, 12, 3, 13, 2, 14, 1, 15)
FARTHEST_FIRST = (7, 5, 3, 6, 1, 4, 2, 0)
X_LINE, X_PLANE, Q_LINE, Q_PLANE, PART_NEAR, PART_FAR, OUT_NEAR, PART_LEAD = range(8)
LEAD_SECTION, LEAD = 0, 1


def nt(left, right):
    return lax.dot_general(
        left, right, (((1,), (1,)), ((), ())), preferred_element_type=F32
    )


def thirds(value):
    first = value.astype(BF16).astype(F32)
    rest = value - first
    second = rest.astype(BF16).astype(F32)
    return first, second, rest - second


def pack_stats(top, total, low, lane):
    slot = lane % (HEAD // 2) // 8
    pieces = thirds(top) + thirds(total)
    tiles = []
    for at in range(0, top.shape[0], 2 * ROWS):
        tile = jnp.zeros(lane.shape, F32)
        for k, piece in enumerate(pieces):
            pair = jnp.where(low, piece[at : at + ROWS], piece[at + ROWS : at + 2 * ROWS])
            tile = jnp.where(slot == k, pair, tile)
        tiles.append(tile.astype(BF16))
    return tiles


def merge(messages):
    stats = []
    for message in messages:
        tile = message[2].astype(F32)
        stats.append(tile + pltpu.roll(tile, HEAD - 8, 1) + pltpu.roll(tile, HEAD - 16, 1))
    top = functools.reduce(jnp.maximum, stats)
    total, sums = 0.0, [0.0, 0.0]
    for message, stat in zip(messages, stats):
        factor = jnp.exp(stat - top)
        total = total + factor * pltpu.roll(stat, HEAD - 24, 1)
        for h in range(2):
            scale = jnp.broadcast_to(factor[:, 64 * h : 64 * h + 1], stat.shape)
            sums[h] = sums[h] + scale * message[h].astype(F32)

    def stacked(stat):
        return jnp.concatenate([stat[:, 0:1], stat[:, 64:65]], axis=0)

    return stacked(top), stacked(total), jnp.concatenate(sums, axis=0)


def kernel(
    x_hbm,
    gain_hbm,
    wq_hbm,
    wo_hbm,
    key_hbm,
    value_hbm,
    scale_hbm,
    owner_hbm,
    number_hbm,
    length_hbm,
    row_hbm,
    freq_hbm,
    out_ref,
    x_own,
    gain,
    wq,
    wo,
    keys,
    values,
    scales,
    owner,
    number,
    length,
    row,
    freq,
    bias,
    turn,
    x_send,
    x_line,
    x_pack,
    x_all,
    q_send,
    q_line,
    q_pack,
    q_all,
    heads,
    part_send,
    part_all,
    sum_send,
    sum_all,
    att_send,
    att_all,
    lead_all,
    local_sem,
    send_sem,
    recv_sem,
    group_sem,
):
    section = lax.axis_index("section")
    tp = lax.axis_index("tp")
    block, mine = tp // NEAR, tp % NEAR
    plane, place = tp // 4, tp % 4
    sections = lax.axis_size("section")
    after = lax.rem(section + 1, sections)
    before = lax.rem(section + sections - 1, sections)

    def near_id(other):
        return {"tp": block * NEAR + other}

    def far_id(other):
        return {"tp": other * NEAR + mine}

    def shifted_near_id(other):
        return {"section": after, "tp": block * NEAR + other}

    def line_id(other):
        return {"tp": other * 4 + place}

    def plane_id(where, other):
        return {"section": where, "tp": plane * 4 + other}

    barrier = pltpu.get_barrier_semaphore()

    def greet(device):
        pl.semaphore_signal(barrier, inc=1, device_id=device, device_id_type=MESH)

    for k in LINE_ORDER:
        greet(line_id(lax.rem(plane + k, PLANES)))
    for k in range(4):
        greet(plane_id(before, k))
    greetings = PLANES - 1 + 4

    moves = [
        pltpu.make_async_copy(src, dst, local_sem.at[k])
        for k, (src, dst) in enumerate(
            [
                (x_hbm, x_own),
                (row_hbm, row),
                (length_hbm, length),
                (owner_hbm, owner),
                (number_hbm, number),
                (scale_hbm, scales),
                (freq_hbm, freq),
                (key_hbm, keys),
                (value_hbm, values),
                (gain_hbm, gain),
                (wq_hbm, wq.at[pl.ds(0, 96)]),
                (wo_hbm, wo),
            ]
        )
    ]
    for move in moves:
        move.start()
    wq[96:128, :] = jnp.zeros((32, wq.shape[1]), BF16)

    moves[0].wait()
    x_here = x_own[...].astype(F32)
    x_send[...] = jnp.concatenate([x_here, x_here], axis=1).astype(BF16)

    lane = lax.broadcasted_iota(I32, (ROWS, HEAD), 1)
    low = lane < HEAD // 2

    def prepare():
        for k in range(1, 7):
            moves[k].wait()
        sub = lax.broadcasted_iota(I32, (ROWS, HEAD), 0)
        row_of = jnp.zeros((ROWS, HEAD), I32)
        limit = jnp.zeros((ROWS, HEAD), I32)
        for r in range(ROWS):
            request = row[0, r]
            row_of = jnp.where(sub == r, request, row_of)
            limit = jnp.where(sub == r, length[0, request], limit)
        for j in range(SLOTS // 2):
            tok_owner = jnp.where(low, owner[0, 2 * j], owner[0, 2 * j + 1])
            tok_page = jnp.where(low, number[0, 2 * j], number[0, 2 * j + 1])
            tok_pos = tok_page * PAGE + lane % PAGE
            seen = (tok_owner == row_of) & (tok_pos < limit)
            bias[:, HEAD * j : HEAD * (j + 1)] = jnp.where(seen, 0.0, MASKED)
        angle = limit.astype(F32) * freq[...]
        turn[0] = jnp.cos(angle)
        sine = jnp.sin(angle)
        turn[1] = jnp.where(low, -sine, sine)

        moves[7].wait()
        moves[8].wait()

        def restore(k, carry):
            at = pl.ds(pl.multiple_of(k * PAGE, PAGE), PAGE)
            both = scales[k]
            for which, store in ((0, keys), (1, values)):
                for g in range(KEY_HEADS):
                    cols = pl.ds(g * HEAD, HEAD)
                    factor = jnp.broadcast_to(both[which : which + 1, g : g + 1], (PAGE, HEAD))
                    store[at, cols] = (store[at, cols].astype(F32) * factor).astype(BF16)
            return carry

        lax.fori_loop(0, SLOTS, restore, 0)
        moves[9].wait()
        moves[10].wait()
        moves[11].wait()

    def send(stage, src, dst, device, sem=None):
        pltpu.make_async_remote_copy(
            src_ref=src,
            dst_ref=dst,
            send_sem=send_sem.at[stage],
            recv_sem=recv_sem.at[stage] if sem is None else sem,
            device_id=device,
            device_id_type=MESH,
        ).start()

    def start_far(stage, src, dst):
        for other in range(BLOCKS):

            @pl.when(block != other)
            def _():
                send(stage, src, dst.at[block], far_id(other))

    chip, core = mine // 2, mine % 2
    sibling = 2 * chip + 1 - core

    lead_group = (section == LEAD_SECTION) & (block == LEAD // NEAR)
    is_lead = lead_group & (mine == LEAD % NEAR)

    def start_near(stage, src, dst):
        for k in FARTHEST_FIRST:
            for c in (0, 1):
                other = 2 * (chip ^ k) + c
                skipped = lead_group & (other == LEAD % NEAR) if c == LEAD % 2 else None
                if k == 0:
                    skipped = core == c if skipped is None else skipped | (core == c)
                if skipped is None:
                    send(stage, src, dst.at[mine], near_id(other))
                else:

                    @pl.when(jnp.logical_not(skipped))
                    def _():
                        send(stage, src, dst.at[mine], near_id(other))

    def line_sem(stage, group):
        return group_sem.at[0 if stage == X_LINE else 1, group]

    def start_line(stage, src, dst):
        for k in LINE_ORDER:
            other = line_id(lax.rem(plane + k, PLANES))
            send(stage, src, dst.at[plane], other, line_sem(stage, block))

    def groups_of_line(stage, buffer):
        for shift in (0, 1, 3, 2):
            group = lax.rem(block + shift, BLOCKS)
            part = buffer.at[pl.ds(0, 4 if shift else 3)]
            pltpu.make_async_remote_copy(
                src_ref=part,
                dst_ref=part,
                send_sem=send_sem.at[stage],
                recv_sem=line_sem(stage, group),
                device_id=near_id(sibling),
                device_id_type=MESH,
            ).wait_recv()
            yield group, [buffer[4 * group + k].astype(F32) for k in range(4)]

    def start_plane(stage, where, src, dst):
        for k in (3, 2, 1, 0):
            send(stage, src, dst, plane_id(where, place ^ k))

    def all_of(stage, part):
        return pltpu.make_async_remote_copy(
            src_ref=part,
            dst_ref=part,
            send_sem=send_sem.at[stage],
            recv_sem=recv_sem.at[stage],
            device_id=near_id(sibling),
            device_id_type=MESH,
        )

    expected = {
        X_LINE: x_line.at[pl.ds(0, PLANES - 1)],
        X_PLANE: x_all,
        Q_LINE: q_line.at[pl.ds(0, PLANES - 1)],
        Q_PLANE: q_all,
        PART_NEAR: part_all,
        PART_FAR: sum_all.at[pl.ds(0, BLOCKS - 1)],
        OUT_NEAR: att_all.at[pl.ds(0, NEAR - 1)],
    }

    def arrived(stage):
        all_of(stage, expected[stage]).wait_recv()

    early = plane < PLANES // 2
    pl.when(early)(prepare)
    pl.semaphore_wait(barrier, greetings)

    start_line(X_LINE, x_send, x_line)
    x_line[plane] = x_send[...]
    pl.when(jnp.logical_not(early))(prepare)
    for group, blocks in groups_of_line(X_LINE, x_line):
        for u in range(2):
            x_pack[group, u] = jnp.where(low, blocks[2 * u], blocks[2 * u + 1]).astype(BF16)
        start_plane(X_PLANE, after, x_pack.at[group], x_all.at[place, group])
    arrived(X_PLANE)

    tiles = [None] * 32
    square = jnp.zeros((ROWS, HEAD), F32)
    for u in range(PLANES // 2):
        for j in range(2):
            even = x_all[2 * j, u // 2, u % 2].astype(F32)
            odd = x_all[2 * j + 1, u // 2, u % 2].astype(F32)
            square = square + even * even + odd * odd
            tiles[4 * u + j] = jnp.where(low, even, pltpu.roll(odd, 64, 1))
            tiles[4 * u + 2 + j] = jnp.where(low, pltpu.roll(even, 64, 1), odd)
    mean = jnp.sum(square, axis=1, keepdims=True) * (1.0 / 4096)
    shrink = lax.rsqrt(mean + 1e-05)
    normed = jnp.concatenate(
        [
            (tiles[t] * shrink * gain[:, HEAD * t : HEAD * (t + 1)]).astype(BF16)
            for t in range(32)
        ],
        axis=1,
    )
    columns = nt(normed, wq[...])
    turned = columns
    for k in range(1, 4):
        turned = jnp.where(place == k, pltpu.roll(columns, 96 * k % 128, 1), turned)
    q_send[...] = turned.astype(BF16)

    start_line(Q_LINE, q_send, q_line)
    q_line[plane] = q_send[...]
    quarter = lane // 32
    for group, blocks in groups_of_line(Q_LINE, q_line):
        for k in range(3):
            moved = pltpu.roll(blocks[3], 96 - 32 * k, 1)
            q_pack[group, k] = jnp.where(quarter == 3 - place, moved, blocks[k]).astype(BF16)
        start_plane(Q_PLANE, before, q_pack.at[group], q_all.at[place, group])
    arrived(Q_PLANE)

    cosine, sine = turn[0], turn[1]
    for c in range(BLOCKS):
        blocks = []
        for p in range(4):
            held = [q_all[p, c, k].astype(F32) for k in range(3)]
            fourth = pltpu.roll(held[0], 32, 1)
            for k in (1, 2):
                moved = pltpu.roll(held[k], 32 * (k + 1), 1)
                fourth = jnp.where(quarter == (4 - p + k) % 4, moved, fourth)
            blocks.append(held + [fourth])
        for z in range(4):
            for k, edge in enumerate((96, 64, 32)):
                h = 3 * (4 * c + z) + k
                head = jnp.where(lane < edge, blocks[k][z], blocks[k + 1][z])
                if h < QUERY_HEADS + KEY_HEADS:
                    head = head * cosine + pltpu.roll(head, 64, 1) * sine
                    head = head.astype(BF16).astype(F32)
                heads[h] = head

    hidden = jnp.concatenate([bias[...]] * 8, axis=0)
    blank = jnp.zeros((4 * ROWS, HEAD), F32)
    for step in (3, 2, 1, 0):
        pair = (chip // 2) ^ step
        cols = pl.ds(pl.multiple_of(pair * 2 * HEAD, 2 * HEAD), 2 * HEAD)
        rows = heads[pl.ds(8 * pair, 8)].reshape(8 * ROWS, HEAD)
        query = jnp.concatenate(
            [
                jnp.concatenate([rows[: 4 * ROWS], blank], axis=1),
                jnp.concatenate([blank, rows[4 * ROWS :]], axis=1),
            ],
            axis=0,
        ).astype(BF16)
        score = nt(query, keys[:, cols]) * SCALE + hidden
        top = jnp.maximum(jnp.max(score, axis=1, keepdims=True), LOWEST)
        weight = jnp.exp(score - top)
        both = jnp.dot(weight.astype(BF16), values[:, cols], preferred_element_type=F32)
        weighted = jnp.concatenate([both[: 4 * ROWS, :HEAD], both[4 * ROWS :, HEAD:]], axis=0)
        total = jnp.sum(weight, axis=1, keepdims=True)
        if step == 0:
            key = QUERY_HEADS + 2 * pair
            new_key = jnp.concatenate([heads[key]] * 4 + [heads[key + 1]] * 4, axis=0)
            key = key + KEY_HEADS
            new_value = jnp.concatenate([heads[key]] * 4 + [heads[key + 1]] * 4, axis=0)
            own = jnp.sum(rows * new_key, axis=1, keepdims=True) * SCALE
            place_of = lax.broadcasted_iota(I32, (8 * ROWS, 1), 0) // (2 * ROWS)
            own = jnp.where((place_of == mine % 4) & (block == 0), own, MASKED)
            peak = jnp.maximum(top, own)
            old_weight, own_weight = jnp.exp(top - peak), jnp.exp(own - peak)
            total = total * old_weight + own_weight
            weighted = weighted * old_weight + own_weight * new_value
            top = peak
        weighted = weighted.astype(BF16)
        for n, stats in enumerate(pack_stats(top, total, low, lane)):
            part_send[4 * pair + n, 0] = weighted[16 * n : 16 * n + 8]
            part_send[4 * pair + n, 1] = weighted[16 * n + 8 : 16 * n + 16]
            part_send[4 * pair + n, 2] = stats
        for n in range(4):
            other = 4 * pair + n
            send(PART_NEAR, part_send.at[other], part_all.at[mine], shifted_near_id(other))

    arrived(PART_NEAR)
    top, total, weighted = merge([part_all[i] for i in range(NEAR)])
    sum_send[0] = weighted[:ROWS].astype(BF16)
    sum_send[1] = weighted[ROWS:].astype(BF16)
    sum_send[2] = pack_stats(top, total, low, lane)[0]

    start_far(PART_FAR, sum_send, sum_all)
    to_lead = (section == LEAD_SECTION) & (tp != LEAD)

    @pl.when(to_lead)
    def _():
        send(PART_LEAD, sum_send, lead_all.at[tp], {"tp": LEAD})

    sum_all[block] = sum_send[...]
    arrived(PART_FAR)
    top, total, weighted = merge([sum_all[c] for c in range(BLOCKS)])
    att_send[...] = (weighted / total).astype(BF16)
    att_all[mine] = att_send[...]
    start_near(OUT_NEAR, att_send, att_all)

    @pl.when(jnp.logical_not(is_lead))
    def _():
        arrived(OUT_NEAR)

    @pl.when(is_lead)
    def _():
        lead_all[LEAD] = sum_send[...]
        all_of(PART_LEAD, lead_all.at[pl.ds(0, BLOCKS * NEAR - 1)]).wait_recv()
        for i in range(NEAR):
            _, total, weighted = merge([lead_all[NEAR * c + i] for c in range(BLOCKS)])
            att_all[i] = (weighted / total).astype(BF16)

    pieces = []
    for i in range(NEAR):
        pair = att_all[i].astype(F32)
        pieces += [pair[:ROWS], pair[ROWS:]]
    attended = jnp.concatenate(pieces, axis=1).astype(BF16)
    x_here = x_all[place, block, plane % 4 // 2].astype(F32)
    x_here = jnp.where(plane % 2 == 0, x_here, pltpu.roll(x_here, 64, 1))[:, :64]
    out_ref[...] = nt(attended, wo[...]) + x_here

    for stage, part in expected.items():
        if stage != OUT_NEAR:
            all_of(stage, part).wait_send()
    fewer = lead_group & jnp.logical_not(is_lead)

    @pl.when(fewer)
    def _():
        all_of(OUT_NEAR, att_all.at[pl.ds(0, NEAR - 2)]).wait_send()

    @pl.when(jnp.logical_not(fewer))
    def _():
        all_of(OUT_NEAR, att_all.at[pl.ds(0, NEAR - 1)]).wait_send()

    @pl.when(to_lead)
    def _():
        all_of(PART_LEAD, sum_send).wait_send()


def local(x, gain, wq, wo, key_codes, value_codes, scale_table, owner, number, lengths, rows):
    half = HEAD // 2
    freq = ROPE_BASE ** (-np.arange(half, dtype=np.float64) / half)
    freq = jnp.asarray(np.concatenate([freq, freq]).astype(np.float32)[None, :])
    operands = (
        x[0],
        gain,
        jnp.swapaxes(wq[0], 0, 1),
        jnp.swapaxes(wo[0], 0, 1),
        key_codes[0].reshape(TOKENS, KEY_HEADS * HEAD),
        value_codes[0].reshape(TOKENS, KEY_HEADS * HEAD),
        scale_table[0],
        owner,
        number,
        lengths,
        rows,
        freq,
    )
    operands = [pltpu.with_memory_space_constraint(x, pltpu.HBM) for x in operands]
    vmem, smem = pltpu.VMEM, pltpu.SMEM
    out = pl.pallas_call(
        kernel,
        out_shape=vmem((ROWS, 64), F32),
        in_specs=[pl.BlockSpec(memory_space=pltpu.HBM)] * len(operands),
        out_specs=pl.BlockSpec(memory_space=pltpu.VMEM),
        scratch_shapes=[
            vmem((ROWS, 64), BF16),
            vmem((1, 4096), F32),
            vmem((128, 4096), BF16),
            vmem((64, 4096), BF16),
            vmem((TOKENS, 1024), BF16),
            vmem((TOKENS, 1024), BF16),
            vmem((SLOTS, 2, KEY_HEADS), F32),
            smem((1, SLOTS), I32),
            smem((1, SLOTS), I32),
            smem((1, 16), I32),
            smem((1, ROWS), I32),
            vmem((1, HEAD), F32),
            vmem((ROWS, TOKENS), F32),
            vmem((2, ROWS, HEAD), F32),
            vmem((ROWS, HEAD), BF16),
            vmem((PLANES, ROWS, HEAD), BF16),
            vmem((BLOCKS, 2, ROWS, HEAD), BF16),
            vmem((4, BLOCKS, 2, ROWS, HEAD), BF16),
            vmem((ROWS, HEAD), BF16),
            vmem((PLANES, ROWS, HEAD), BF16),
            vmem((BLOCKS, 3, ROWS, HEAD), BF16),
            vmem((4, BLOCKS, 3, ROWS, HEAD), BF16),
            vmem((HEADS, ROWS, HEAD), F32),
            vmem((NEAR, 3, ROWS, HEAD), BF16),
            vmem((NEAR, 3, ROWS, HEAD), BF16),
            vmem((3, ROWS, HEAD), BF16),
            vmem((BLOCKS, 3, ROWS, HEAD), BF16),
            vmem((2 * ROWS, HEAD), BF16),
            vmem((NEAR, 2 * ROWS, HEAD), BF16),
            vmem((BLOCKS * NEAR, 3, ROWS, HEAD), BF16),
            pltpu.SemaphoreType.DMA((12,)),
            pltpu.SemaphoreType.DMA((8,)),
            pltpu.SemaphoreType.DMA((8,)),
            pltpu.SemaphoreType.DMA((2, BLOCKS)),
        ],
        compiler_params=pltpu.CompilerParams(
            collective_id=0, has_side_effects=True, vmem_limit_bytes=40 * 2**20
        ),
    )(*operands)
    return out[None]


def solution(mesh):
    in_specs = (
        P("section", None, "tp"),
        P("section", None),
        P("section", None, "tp"),
        P("section", None, "tp"),
        P("section", "tp", None, None),
        P("section", "tp", None, None),
        P("section", "tp", None, None),
        P("section", "tp"),
        P("section", "tp"),
        P("section", None),
        P("section", None),
    )
    out_specs = P("section", None, "tp")
    return jax.shard_map(local, mesh=mesh, in_specs=in_specs, out_specs=out_specs, check_vma=False)
```
